32 devices in a mesh: group: 4 (over z), dev: 8 (over y, x, core).
Axes of the slice: x: 2, y: 2, z: 4, core: 2. Of those that a mesh axis runs over, the one named last changes fastest.
Arguments:
- corpus_tokens: bfloat16 [4096, 1024], P(('group', 'dev')), may hold values from -6 to 6
- norm_gain: float32 [1024], replicated, may hold values from 0.1 to 1.9
- wi_weight: bfloat16 [1024, 5248], P('dev'), may hold values from -0.1875 to 0.1875
- wo_weight: bfloat16 [2624, 1024], P('dev'), may hold values from -0.125 to 0.125
- final_gain: float32 [1024], replicated, may hold values from 0.1 to 1.9
- proj_weight: bfloat16 [1024, 128], replicated, may hold values from -0.1875 to 0.1875
- query_vectors: bfloat16 [64, 32, 128], P(('group', 'dev')), may hold values from -6 to 6
- doc_lengths: int32 [4, 4], P('group'), may hold values from 1 to 512, 1024 in all within a row
- candidates: int32 [64, 100], P(('group', 'dev')), may hold values from 0 to 15
Outputs:
- doc_vectors: bfloat16 [4096, 128], P(('group', 'dev'))
- scores: float32 [64, 100], P(('group', 'dev'))
The draws below stay inside these ranges and needn't reach their ends.
Inputs may be any that keep to these rules, and one draw needn't show every extreme that they name: `doc_lengths`: each row sums to 1024; its largest length is exactly 512. `candidates`: document k of group g has id g * 4 + k; ids may repeat within a row.
All inputs are finite; a program needn't handle non-finite values.
Results may differ from the reference program's by a relative error of at most 0.0062.
Values may be sent and summed in bfloat16 or wider, within the bound.
No kernel may reach another device: no remote copies, remote signals or barrier semaphores. Data moves between devices by JAX's collectives and lax.ppermute only.
A program may use at most 128 MiB of HBM per device.

```python
import math
import jax
import jax.numpy as jnp
import numpy as np
from jax import lax

D = 1024
FF = 2624
DIM = 128
QT = 32
NCAND = 100
DOCS_G = 4
SHARD = 1024
DOC_MOST = 512
TOKENS = 4096
NDOCS = 16
NQ = 64
N_GROUP = 4


def place_ends(entries, rng, low, largest):
    longest = entries.shape.index(max(entries.shape))
    spots = []
    for shift in (0, 1):
        where = [jax.random.randint(jax.random.fold_in(rng, axis), (), 0, length) for axis, length in enumerate(entries.shape)]
        where[longest] = (where[longest] + shift) % entries.shape[longest]
        spots.append(tuple(where))
    return entries.at[spots[0]].set(low).at[spots[1]].set(largest)


def block_scale(rng, shape, shards, smallest, top_value):
    loudness, own = 1.0, jax.random.fold_in(rng, 6)
    for dim, shards_of in shards:
        heights = jnp.exp(jax.random.uniform(jax.random.fold_in(own, dim), (shards_of,), jnp.float32, smallest / len(shards), top_value / len(shards)))
        loudness = loudness * jnp.repeat(heights, shape[dim] // shards_of).reshape([-1 if axis == dim else 1 for axis in range(len(shape))])
    return loudness


def cumulative_ranks(amount, slope):
    portions = [(1 << 20) // math.isqrt(standing ** slope) + 1 for standing in range(1, amount + 1)]
    scale = 1 + sum(portions) // (1 << 30)
    return np.cumsum(np.array([max(1, weight // scale) for weight in portions]))


def ranked_ids(own_key, extent, amount, lean):
    table = cumulative_ranks(amount, lean)
    lot = jax.random.randint(jax.random.fold_in(own_key, 1), extent, 0, int(table[amount - 1]))
    rank = jnp.searchsorted(jnp.asarray(table, jnp.int32), lot, side="right")
    return jax.random.permutation(jax.random.fold_in(own_key, 2), amount)[rank].astype(jnp.int32)


def split_up(amount, total, limit, lean):
    loads = [(1 << 20) // math.isqrt(standing ** lean) + 1 for standing in range(2, amount + 1)]
    rest, counts = total - limit - (amount - 1), [1] * (amount - 1)
    while rest > 0:
        movable = [i for i in range(amount - 1) if counts[i] < limit]
        mass, budget = sum([loads[i] for i in movable]), rest
        for i in movable:
            more = min(limit - counts[i], max(1, budget * loads[i] // mass), rest)
            counts[i] = counts[i] + more
            rest = rest - more
    return np.array([limit] + counts)


def uneven_parts(own_key, amount, total, bound, lean):
    if amount == 2:
        one = jax.random.randint(own_key, (), max(1, total - bound), min(bound, total - 1) + 1)
        return jnp.stack([one, total - one])
    tallies = jnp.asarray(split_up(amount, total, bound, lean), jnp.int32)
    couples = (amount - 1) // 2
    giver, receiver = tallies[1:1 + 2 * couples:2], tallies[2:2 + 2 * couples:2]
    margin = jnp.minimum(giver - 1, bound - receiver)
    shifted = jax.random.randint(jax.random.fold_in(own_key, 1), (couples,), 0, 1 << 20) % (margin + 1)
    tallies = tallies.at[1:1 + 2 * couples:2].set(giver - shifted).at[2:2 + 2 * couples:2].set(receiver + shifted)
    return tallies[jax.random.permutation(jax.random.fold_in(own_key, 2), amount)]


def centred(own_key, extent, deviation, most, split=(), kind=jnp.bfloat16):
    array = deviation * jax.random.normal(own_key, extent, jnp.float32)
    if split:
        array = array * block_scale(own_key, extent, split, -0.22, 0.18)
    return jnp.clip(array, -most, most).astype(kind)


def setup_inputs(seed: int = 0) -> dict:
    seeds = jax.random.split(jax.random.key(seed), 10)
    corpus_tokens = centred(seeds[0], (TOKENS, D), 1.0, 6.0, ((0, 32),))
    norm_gain = jnp.clip(1.0 + 0.18 * jax.random.normal(seeds[1], (D,), jnp.float32), 0.1, 1.9)
    wi_weight = centred(seeds[2], (D, 2 * FF), D ** -0.5, 0.1875, ((0, 8),))
    wo_weight = centred(seeds[3], (FF, D), FF ** -0.5, 0.125, ((0, 8),))
    final_gain = jnp.clip(1.0 + 0.18 * jax.random.normal(seeds[4], (D,), jnp.float32), 0.1, 1.9)
    proj_weight = centred(seeds[5], (D, DIM), D ** -0.5, 0.1875)
    query_vectors = centred(seeds[6], (NQ, QT, DIM), 1.0, 6.0, ((0, 32),))
    doc_lengths = jax.vmap(lambda own: uneven_parts(own, DOCS_G, SHARD, DOC_MOST, 2))(jax.random.split(seeds[7], N_GROUP)).reshape((N_GROUP, DOCS_G)).astype(jnp.int32)
    candidates = place_ends(ranked_ids(seeds[8], (NQ, NCAND), NDOCS, 2), jax.random.fold_in(seeds[8], 3), 0, NDOCS - 1).astype(jnp.int32)
    return {"corpus_tokens": corpus_tokens, "norm_gain": norm_gain, "wi_weight": wi_weight, "wo_weight": wo_weight, "final_gain": final_gain, "proj_weight": proj_weight, "query_vectors": query_vectors, "doc_lengths": doc_lengths, "candidates": candidates}


def layer_norm(values, gain_row):
    values = values.astype(jnp.float32)
    center = lax.optimization_barrier(jnp.mean(values, axis=-1, keepdims=True))
    spread = lax.optimization_barrier(jnp.mean(jnp.square(values - center), axis=-1, keepdims=True))
    return (values - center) * lax.rsqrt(spread + 1e-05) * gain_row.astype(jnp.float32)

def encode(tokens, norm_gain, wi_weight, wo_weight, final_gain, proj_weight):
    normed = layer_norm(tokens, norm_gain).astype(jnp.bfloat16)
    lifted = jnp.dot(normed, wi_weight, preferred_element_type=jnp.float32)
    hidden_width = wo_weight.shape[0]
    hidden = (jax.nn.gelu(lifted[:, :hidden_width], approximate=False) * lifted[:, hidden_width:]).astype(jnp.bfloat16)
    mixed_sum = tokens.astype(jnp.float32) + jnp.dot(hidden, wo_weight, preferred_element_type=jnp.float32)
    normed_out = layer_norm(mixed_sum, final_gain).astype(jnp.bfloat16)
    projected = jnp.dot(normed_out, proj_weight, preferred_element_type=jnp.float32)
    inverse = lax.rsqrt(lax.optimization_barrier(jnp.sum(projected * projected, axis=-1, keepdims=True)) + 1e-06)
    return (projected * inverse).astype(jnp.bfloat16)

def document_of(lengths, total_rows):
    doc_ends = jnp.cumsum(lengths.astype(jnp.int32))
    places = jnp.arange(total_rows, dtype=jnp.int32)
    return lax.optimization_barrier(jnp.sum((places[:, None] >= doc_ends[None, :]).astype(jnp.int32), axis=1))

def group_maxima(query_rows, vectors, owners):
    row_block = math.gcd(vectors.shape[0], 2048)
    count_steps = vectors.shape[0] // row_block
    start_value = jnp.full((DOCS_G, query_rows.shape[0]), -jnp.inf, jnp.bfloat16)

    def advance(running, element):
        vector_part, owner_part = element
        similar = jnp.dot(vector_part, query_rows.T, preferred_element_type=jnp.float32).astype(jnp.bfloat16)
        return (running.at[owner_part].max(similar), None)
    outcome, _ = lax.scan(advance, start_value, (vectors.reshape(count_steps, row_block, vectors.shape[1]), owners.reshape(count_steps, row_block)))
    return outcome

def reference(corpus_tokens, norm_gain, wi_weight, wo_weight, final_gain, proj_weight, query_vectors, doc_lengths, candidates):
    grouped = corpus_tokens.reshape(N_GROUP, SHARD, D)
    vectors = lax.map(lambda group_rows: encode(group_rows, norm_gain, wi_weight, wo_weight, final_gain, proj_weight), grouped)
    query_rows = query_vectors.reshape(NQ * QT, DIM)
    owners = jax.vmap(lambda lengths: document_of(lengths, SHARD))(doc_lengths)
    maxima = lax.map(lambda group_pair: group_maxima(query_rows, group_pair[0], group_pair[1]), (vectors, owners))
    doc_scores = lax.optimization_barrier(jnp.sum(maxima.astype(jnp.float32).reshape(N_GROUP, DOCS_G, NQ, QT), axis=-1)) / QT
    score_table = jnp.transpose(doc_scores, (2, 0, 1)).reshape(NQ, NDOCS)
    scores = jnp.take_along_axis(score_table, candidates.astype(jnp.int32), axis=1)
    return (vectors.reshape(TOKENS, DIM), scores)
```

```python
import functools

import jax
import jax.numpy as jnp
from jax import lax
from jax.experimental import pallas as pl
from jax.experimental.pallas import tpu as pltpu
from jax.sharding import PartitionSpec as P

VMEM_LIMIT = 48 * 1024 * 1024


def norm_rows(values, gain_row):
    center = jnp.mean(values, axis=-1, keepdims=True)
    shifted = values - center
    spread = jnp.mean(shifted * shifted, axis=-1, keepdims=True)
    return (shifted * lax.rsqrt(spread + 1e-05) * gain_row).astype(jnp.bfloat16)


def dot_nt(left, right):
    return lax.dot_general(
        left, right, (((1,), (1,)), ((), ())), preferred_element_type=jnp.float32
    )


def split_kernel(chips, place_ref, wi_ref, *refs):
    pieces, turned = refs[:chips], refs[chips]
    columns = wi_ref.shape[1]
    width = columns // 2
    part = width // chips
    chip = place_ref[0]
    for start in range(0, columns, 128):
        turned[start : start + 128, :] = wi_ref[:, start : start + 128].T
    for step in range(chips):
        target = chip ^ step
        for half in range(2):
            first = pl.multiple_of(half * width + target * part, 16)
            pieces[step][half] = turned[pl.ds(first, part), :]


def ffn_kernel(chips, pieces, place_ref, gain_ref, wo_ref, *refs):
    tokens, refs = refs[:chips], refs[chips:]
    if pieces:
        mine, other, outs = refs[:pieces], refs[pieces : 2 * pieces], refs[2 * pieces : -2]
    else:
        outs, refs = refs[2:], refs[:2]
    gelu_w, gate_w = refs[-2:]
    chip, core = place_ref[0], place_ref[1]
    for step in range(pieces):
        source = (chip ^ step) * 2
        for block, at in ((mine[step], source + core), (other[step], source + 1 - core)):
            columns = pl.ds(pl.multiple_of(at * 128, 128), 128)
            gelu_w[:, columns] = block[0]
            gate_w[:, columns] = block[1]
    for step in list(range(1, chips)) + [0]:
        normed = norm_rows(tokens[step][...].astype(jnp.float32), gain_ref[...])
        first = dot_nt(normed, gelu_w[...])
        second = dot_nt(normed, gate_w[...])
        hidden = (0.5 * first * (1.0 + lax.erf(first * 0.7071067811865476)) * second).astype(jnp.bfloat16)
        outs[step][...] = jnp.dot(hidden, wo_ref[...], preferred_element_type=jnp.float32).astype(
            outs[step].dtype
        )


def finish_kernel(chips, tokens_ref, gain_ref, proj_ref, own_ref, *refs):
    mixed = tokens_ref[...].astype(jnp.float32) + own_ref[...]
    for step in range(chips - 1):
        mixed = mixed + refs[step][...].astype(jnp.float32)
    final = norm_rows(mixed, gain_ref[...])
    projected = jnp.dot(final, proj_ref[...], preferred_element_type=jnp.float32)
    total = jnp.sum(projected * projected, axis=-1, keepdims=True)
    refs[chips - 1][...] = (projected * lax.rsqrt(total + 1e-06)).astype(jnp.bfloat16)


def score_kernel(devices, docs, query_len, place_ref, ends_ref, query_ref, *refs):
    blocks, out_ref = refs[:devices], refs[devices]
    me = place_ref[0]
    rows = blocks[0].shape[0]
    query_rows = query_ref.shape[0]
    queries = query_rows // query_len
    best = [jnp.full((1, query_rows), -jnp.inf, jnp.float32) for _ in range(docs)]
    for step in range(devices):
        similar = dot_nt(blocks[step][...], query_ref[...])
        spot = (me ^ step) * rows + lax.broadcasted_iota(jnp.int32, similar.shape, 0)
        low = jnp.int32(0)
        for doc in range(docs):
            high = ends_ref[doc]
            inside = (spot >= low) & (spot < high)
            masked = jnp.where(inside, similar, -jnp.inf)
            best[doc] = jnp.maximum(best[doc], jnp.max(masked, axis=0, keepdims=True))
            low = high
    maxima = jnp.concatenate(best, axis=0).astype(jnp.bfloat16)
    row = lax.broadcasted_iota(jnp.int32, (query_rows, queries), 0) // query_len
    column = lax.broadcasted_iota(jnp.int32, (query_rows, queries), 1)
    member = (row == column).astype(jnp.bfloat16)
    out_ref[...] = jnp.dot(maxima, member, preferred_element_type=jnp.float32) / query_len


def body(
    corpus_tokens,
    norm_gain,
    wi_weight,
    wo_weight,
    final_gain,
    proj_weight,
    query_vectors,
    doc_lengths,
    candidates,
):
    groups = lax.axis_size("group")
    devices = lax.axis_size("dev")
    chips = devices // 2
    rows, width = corpus_tokens.shape
    part = wo_weight.shape[0] * 2
    me = lax.axis_index("dev").astype(jnp.int32)
    place = jnp.stack([me // 2, me % 2])
    smem = pl.BlockSpec(memory_space=pltpu.SMEM)
    vmem = pl.BlockSpec(memory_space=pltpu.VMEM)
    params = pltpu.CompilerParams(vmem_limit_bytes=VMEM_LIMIT)

    def swap(values, mask, axis="dev"):
        size = devices if axis == "dev" else groups
        return lax.ppermute(values, axis, [(i, i ^ mask) for i in range(size)])

    tokens = [corpus_tokens] + [swap(corpus_tokens, 2 * step) for step in range(1, chips)]
    if wi_weight.shape[0] == 128 and part % 16 == 0:
        pieces = pl.pallas_call(
            functools.partial(split_kernel, chips),
            out_shape=[jax.ShapeDtypeStruct((2, part, 128), jnp.bfloat16)] * chips,
            in_specs=[smem, vmem],
            out_specs=[vmem] * chips,
            scratch_shapes=[pltpu.VMEM((wi_weight.shape[1], 128), jnp.bfloat16)],
            compiler_params=params,
        )(place, wi_weight)
        mine = [pieces[0]] + [swap(pieces[step], 2 * step) for step in range(1, chips)]
        other = [swap(piece, 1) for piece in mine]
        weights = mine + other
        scratch = [pltpu.VMEM((part, width), jnp.bfloat16)] * 2
    else:
        whole = lax.all_gather(wi_weight, "dev", axis=0, tiled=True).reshape(width, 2, chips, part)
        columns = lax.dynamic_index_in_dim(whole, me // 2, 2, keepdims=False)
        weights = [columns[:, half].T for half in range(2)]
        scratch = []
    wo_other = swap(wo_weight, 1)
    even = (me % 2) == 0
    wo_part = jnp.concatenate(
        [jnp.where(even, wo_weight, wo_other), jnp.where(even, wo_other, wo_weight)], axis=0
    )
    query_own = query_vectors
    queries = [query_own] + [swap(query_own, mask, "group") for mask in range(1, groups)]
    query_rows = jnp.concatenate([each.reshape(-1, each.shape[-1]) for each in queries], axis=0)

    partial = pl.pallas_call(
        functools.partial(ffn_kernel, chips, len(weights) // 2 if scratch else 0),
        out_shape=[
            jax.ShapeDtypeStruct((rows, width), jnp.float32 if step == 0 else jnp.bfloat16)
            for step in range(chips)
        ],
        in_specs=[smem, vmem, vmem] + [vmem] * (chips + len(weights)),
        out_specs=[vmem] * chips,
        scratch_shapes=scratch,
        compiler_params=params,
    )(place, norm_gain.reshape(1, -1), wo_part, *tokens, *weights)
    arrived = [swap(partial[step], 2 * step) for step in range(1, chips)]
    vectors = pl.pallas_call(
        functools.partial(finish_kernel, chips),
        out_shape=jax.ShapeDtypeStruct((rows, proj_weight.shape[1]), jnp.bfloat16),
        in_specs=[vmem] * (4 + chips - 1),
        out_specs=vmem,
        compiler_params=params,
    )(corpus_tokens, final_gain.reshape(1, -1), proj_weight, partial[0], *arrived)

    blocks = [vectors] + [swap(vectors, mask) for mask in range(1, devices)]
    docs = doc_lengths.shape[1]
    per_query, query_len, _ = query_vectors.shape
    table = pl.pallas_call(
        functools.partial(score_kernel, devices, docs, query_len),
        out_shape=jax.ShapeDtypeStruct((docs, groups * per_query), jnp.float32),
        in_specs=[smem, smem, vmem] + [vmem] * devices,
        out_specs=vmem,
        compiler_params=params,
    )(me.reshape(1), jnp.cumsum(doc_lengths[0]), query_rows, *blocks)
    sent = [table[:, mask * per_query : (mask + 1) * per_query] for mask in range(groups)]
    got = [sent[0]] + [swap(sent[mask], mask, "group") for mask in range(1, groups)]
    home = lax.axis_index("group").astype(jnp.int32)
    scores = jnp.zeros(candidates.shape, jnp.float32)
    for mask in range(groups):
        for doc in range(docs):
            wanted = (home ^ mask) * docs + doc
            scores = jnp.where(candidates == wanted, got[mask][doc][:, None], scores)
    return (vectors, scores)


def solution(mesh):
    placed = (
        P(("group", "dev"), None),
        P(),
        P("dev", None),
        P("dev", None),
        P(),
        P(),
        P(("group", "dev"), None, None),
        P("group", None),
        P(("group", "dev"), None),
    )
    return jax.shard_map(
        body,
        mesh=mesh,
        in_specs=placed,
        out_specs=(P(("group", "dev"), None), P(("group", "dev"), None)),
        check_vma=False,
    )
```

```python
import functools

import jax
import jax.numpy as jnp
from jax import lax
from jax.experimental import pallas as pl
from jax.experimental.pallas import tpu as pltpu
from jax.sharding import PartitionSpec as P

VMEM_LIMIT = 20 * 1024 * 1024


def norm_rows(values, gain_row):
    center = jnp.mean(values, axis=-1, keepdims=True)
    shifted = values - center
    spread = jnp.mean(shifted * shifted, axis=-1, keepdims=True)
    return (shifted * lax.rsqrt(spread + 1e-05) * gain_row).astype(jnp.bfloat16)


def dot_nt(left, right):
    return lax.dot_general(
        left, right, (((1,), (1,)), ((), ())), preferred_element_type=jnp.float32
    )


def split_kernel(chips, place_ref, wi_ref, *refs):
    pieces, turned = refs[:chips], refs[chips]
    columns = wi_ref.shape[1]
    width = columns // 2
    part = width // chips
    chip = place_ref[0]
    for start in range(0, columns, 128):
        turned[start : start + 128, :] = wi_ref[:, start : start + 128].T
    for step in range(chips):
        target = chip ^ step
        for half in range(2):
            first = pl.multiple_of(half * width + target * part, 16)
            pieces[step][half] = turned[pl.ds(first, part), :]


def join_kernel(chips, place_ref, wo_mine, wo_other, *refs):
    mine, other = refs[:chips], refs[chips : 2 * chips]
    gelu_w, gate_w, wo_part = refs[2 * chips :]
    chip, core = place_ref[0], place_ref[1]
    rows = wo_mine.shape[0]
    for first, upper, lower in ((0, wo_mine, wo_other), (1, wo_other, wo_mine)):

        @pl.when(core == first)
        def _(upper=upper, lower=lower):
            wo_part[:rows] = upper[...]
            wo_part[rows:] = lower[...]

    for step in range(chips):
        source = (chip ^ step) * 2
        for block, at in ((mine[step], source + core), (other[step], source + 1 - core)):
            columns = pl.ds(pl.multiple_of(at * 128, 128), 128)
            gelu_w[:, columns] = block[0]
            gate_w[:, columns] = block[1]


def ffn_kernel(gain_ref, gelu_w, gate_w, wo_part, tokens_ref, out_ref):
    normed = norm_rows(tokens_ref[...].astype(jnp.float32), gain_ref[...])
    first = dot_nt(normed, gelu_w[...])
    second = dot_nt(normed, gate_w[...])
    hidden = (0.5 * first * (1.0 + lax.erf(first * 0.7071067811865476)) * second).astype(jnp.bfloat16)
    out_ref[...] = jnp.dot(hidden, wo_part[...], preferred_element_type=jnp.float32).astype(
        out_ref.dtype
    )


def finish_kernel(chips, docs, place_ref, ends_ref, tokens_ref, gain_ref, proj_ref, own_ref, *refs):
    parts, refs = refs[: chips - 1], refs[chips - 1 :]
    queries, (vectors_ref, out_ref) = refs[:-2], refs[-2:]
    mixed = tokens_ref[...].astype(jnp.float32) + own_ref[...]
    for part in parts:
        mixed = mixed + part[...].astype(jnp.float32)
    final = norm_rows(mixed, gain_ref[...])
    projected = jnp.dot(final, proj_ref[...], preferred_element_type=jnp.float32)
    total = jnp.sum(projected * projected, axis=-1, keepdims=True)
    vectors = (projected * lax.rsqrt(total + 1e-06)).astype(jnp.bfloat16)
    vectors_ref[...] = vectors
    group, me = place_ref[0], place_ref[1]
    devices = 2 * chips
    rows = vectors.shape[0]
    block_rows = queries[0].shape[0]
    groups = out_ref.shape[0] // devices
    together = 128 // (block_rows // groups)
    spot = me * rows + lax.broadcasted_iota(jnp.int32, (rows, block_rows), 0)
    inside, low = [], jnp.int32(0)
    for doc in range(docs):
        high = ends_ref[doc]
        inside.append((spot >= low) & (spot < high))
        low = high
    for mask, block in enumerate(queries):
        similar = dot_nt(vectors, block[...])
        best = [
            jnp.max(jnp.where(inside[doc], similar, -jnp.inf), axis=0, keepdims=True)
            for doc in range(docs)
        ]
        best = jnp.concatenate(best, axis=0).astype(jnp.bfloat16)
        for far in range(groups):
            tile = far // together
            out_ref[(group ^ far) * devices + (me ^ mask)] = best[:, tile * 128 : (tile + 1) * 128]


def pick_kernel(query_len, place_ref, cand_ref, best_ref, out_ref):
    group = place_ref[0]
    groups, devices, docs, lanes = best_ref.shape
    own, listed = cand_ref.shape
    together = lanes // (own * query_len)
    scores = [jnp.zeros((1, listed), jnp.float32) for _ in range(own)]
    lane = lax.broadcasted_iota(jnp.int32, (docs, lanes), 1)
    label = lax.broadcasted_iota(jnp.int32, (docs, listed), 0)
    for far in range(groups):
        best = jnp.max(best_ref[far].astype(jnp.float32), axis=0)
        offset = ((group ^ far) % together) * own * query_len
        for query in range(own):
            start = offset + query * query_len
            taken = jnp.where((lane >= start) & (lane < start + query_len), best, 0.0)
            value = jnp.sum(taken, axis=1, keepdims=True) / query_len
            wanted = cand_ref[query : query + 1, :] - far * docs
            scores[query] += jnp.sum(jnp.where(wanted == label, value, 0.0), axis=0, keepdims=True)
    for query in range(own):
        out_ref[query : query + 1, :] = scores[query]


def body(
    corpus_tokens,
    norm_gain,
    wi_weight,
    wo_weight,
    final_gain,
    proj_weight,
    query_vectors,
    doc_lengths,
    candidates,
):
    groups = lax.axis_size("group")
    devices = lax.axis_size("dev")
    chips = devices // 2
    rows, width = corpus_tokens.shape
    part = wo_weight.shape[0] * 2
    me = lax.axis_index("dev").astype(jnp.int32)
    place = jnp.stack([me // 2, me % 2])
    smem = pl.BlockSpec(memory_space=pltpu.SMEM)
    vmem = pl.BlockSpec(memory_space=pltpu.VMEM)
    params = pltpu.CompilerParams(vmem_limit_bytes=VMEM_LIMIT)

    def swap(values, mask, axis="dev"):
        size = devices if axis == "dev" else groups
        return lax.ppermute(values, axis, [(i, i ^ mask) for i in range(size)])

    per_query, query_len, vector_dim = query_vectors.shape
    query_own = query_vectors.reshape(-1, vector_dim)
    wo_other = swap(wo_weight, 1)
    tokens = [corpus_tokens] + [swap(corpus_tokens, 2 * step) for step in range(1, chips)]
    weight_shapes = [
        jax.ShapeDtypeStruct((part, width), jnp.bfloat16),
        jax.ShapeDtypeStruct((part, width), jnp.bfloat16),
        jax.ShapeDtypeStruct((part, wo_weight.shape[1]), jnp.bfloat16),
    ]
    if wi_weight.shape[0] == 128 and part % 16 == 0:
        pieces = pl.pallas_call(
            functools.partial(split_kernel, chips),
            out_shape=[jax.ShapeDtypeStruct((2, part, 128), jnp.bfloat16)] * chips,
            in_specs=[smem, vmem],
            out_specs=[vmem] * chips,
            scratch_shapes=[pltpu.VMEM((wi_weight.shape[1], 128), jnp.bfloat16)],
            compiler_params=params,
        )(place, wi_weight)
        mine = [pieces[0]] + [swap(pieces[step], 2 * step) for step in range(1, chips)]
        mine[1], tokens[1], tokens[2], query_own = lax.optimization_barrier(
            (mine[1], tokens[1], tokens[2], query_own)
        )
        other = [swap(piece, 1) for piece in mine]
        weights = pl.pallas_call(
            functools.partial(join_kernel, chips),
            out_shape=weight_shapes,
            in_specs=[smem] + [vmem] * (2 + 2 * chips),
            out_specs=[vmem] * 3,
            compiler_params=params,
        )(place, wo_weight, wo_other, *mine, *other)
    else:
        whole = lax.all_gather(wi_weight, "dev", axis=0, tiled=True).reshape(width, 2, chips, part)
        columns = lax.dynamic_index_in_dim(whole, me // 2, 2, keepdims=False)
        even = (me % 2) == 0
        wo_part = jnp.concatenate(
            [jnp.where(even, wo_weight, wo_other), jnp.where(even, wo_other, wo_weight)], axis=0
        )
        weights = [columns[:, 0].T, columns[:, 1].T, wo_part]

    line = jnp.concatenate(
        [query_own] + [swap(query_own, mask, "group") for mask in range(1, groups)], axis=0
    )
    plane = jnp.stack([line] + [swap(line, 2 * step) for step in range(1, chips)])
    beside = swap(plane, 1)
    queries = [(plane, beside)[mask % 2][mask // 2] for mask in range(devices)]

    partial = [None] * chips
    for step in list(range(1, chips)) + [0]:
        partial[step] = pl.pallas_call(
            ffn_kernel,
            out_shape=jax.ShapeDtypeStruct((rows, width), jnp.bfloat16 if step else jnp.float32),
            in_specs=[vmem] * 5,
            out_specs=vmem,
            compiler_params=params,
        )(norm_gain.reshape(1, -1), *weights, tokens[step])
    arrived = [swap(partial[step], 2 * step) for step in range(1, chips)]

    docs = doc_lengths.shape[1]
    home = jnp.stack([lax.axis_index("group").astype(jnp.int32), me])
    vectors, best = pl.pallas_call(
        functools.partial(finish_kernel, chips, docs),
        out_shape=[
            jax.ShapeDtypeStruct((rows, proj_weight.shape[1]), jnp.bfloat16),
            jax.ShapeDtypeStruct((groups * devices, docs, 128), jnp.bfloat16),
        ],
        in_specs=[smem, smem] + [vmem] * (4 + chips - 1 + devices),
        out_specs=[vmem, vmem],
        compiler_params=params,
    )(
        home,
        jnp.cumsum(doc_lengths[0]),
        corpus_tokens,
        final_gain.reshape(1, -1),
        proj_weight,
        partial[0],
        *arrived,
        *queries,
    )
    met = lax.all_to_all(best, ("group", "dev"), split_axis=0, concat_axis=0, tiled=True)
    scores = pl.pallas_call(
        functools.partial(pick_kernel, query_len),
        out_shape=jax.ShapeDtypeStruct(candidates.shape, jnp.float32),
        in_specs=[smem, vmem, vmem],
        out_specs=vmem,
        compiler_params=params,
    )(home, candidates, met.reshape(groups, devices, docs, 128))
    return (vectors, scores)


def solution(mesh):
    placed = (
        P(("group", "dev"), None),
        P(),
        P("dev", None),
        P("dev", None),
        P(),
        P(),
        P(("group", "dev"), None, None),
        P("group", None),
        P(("group", "dev"), None),
    )
    return jax.shard_map(
        body,
        mesh=mesh,
        in_specs=placed,
        out_specs=(P(("group", "dev"), None), P(("group", "dev"), None)),
        check_vma=False,
    )
```

```python
import functools

import jax
import jax.numpy as jnp
from jax import lax
from jax.experimental import pallas as pl
from jax.experimental.pallas import tpu as pltpu
from jax.sharding import PartitionSpec as P

VMEM_LIMIT = 20 * 1024 * 1024


def norm_rows(values, gain_row):
    center = jnp.mean(values, axis=-1, keepdims=True)
    shifted = values - center
    spread = jnp.mean(shifted * shifted, axis=-1, keepdims=True)
    return (shifted * lax.rsqrt(spread + 1e-05) * gain_row).astype(jnp.bfloat16)


def dot_nt(left, right):
    return lax.dot_general(
        left, right, (((1,), (1,)), ((), ())), preferred_element_type=jnp.float32
    )


def split_kernel(chips, wi_ref, query_ref, *refs):
    pieces, turned = refs[:chips], refs[chips]
    columns = wi_ref.shape[1]
    width = columns // 2
    part = width // chips
    chip = lax.axis_index("dev") // 2
    for start in range(0, columns, 128):
        turned[start : start + 128, :] = wi_ref[:, start : start + 128].T
    for step in range(chips):
        for half in range(2):
            first = pl.multiple_of(half * width + (chip ^ step) * part, 16)
            pieces[step][half * part : (half + 1) * part] = turned[pl.ds(first, part), :]
        pieces[step][2 * part :] = query_ref[...]


def join_kernel(chips, wo_mine, wo_other, *refs):
    mine, other = refs[:chips], refs[chips : 2 * chips]
    gelu_w, gate_w, wo_part, queries = refs[2 * chips :]
    chip, core = lax.axis_index("dev") // 2, lax.axis_index("dev") % 2
    rows = wo_mine.shape[0]
    for first, upper, lower in ((0, wo_mine, wo_other), (1, wo_other, wo_mine)):

        @pl.when(core == first)
        def _(upper=upper, lower=lower):
            wo_part[:rows] = upper[...]
            wo_part[rows:] = lower[...]

    part = gelu_w.shape[0]
    own = mine[0].shape[0] - 2 * part
    for step in range(chips):
        source = (chip ^ step) * 2
        for block, at in ((mine[step], source + core), (other[step], source + 1 - core)):
            columns = pl.ds(pl.multiple_of(at * 128, 128), 128)
            gelu_w[:, columns] = block[:part]
            gate_w[:, columns] = block[part : 2 * part]
            queries[pl.ds(pl.multiple_of(at * own, own), own), :] = block[2 * part :]


def ffn_kernel(gain_ref, gelu_w, gate_w, wo_part, tokens_ref, out_ref):
    normed = norm_rows(tokens_ref[...].astype(jnp.float32), gain_ref[...])
    first = dot_nt(normed, gelu_w[...])
    second = dot_nt(normed, gate_w[...])
    hidden = (0.5 * first * (1.0 + lax.erf(first * 0.7071067811865476)) * second).astype(jnp.bfloat16)
    out_ref[...] = jnp.dot(hidden, wo_part[...], preferred_element_type=jnp.float32).astype(
        out_ref.dtype
    )


def finish_kernel(chips, lengths_ref, tokens_ref, gain_ref, proj_ref, own_ref, *refs):
    parts, refs = refs[: chips - 1], refs[chips - 1 :]
    queries, (vectors_ref, out_ref) = refs[:-2], refs[-2:]
    mixed = tokens_ref[...].astype(jnp.float32) + own_ref[...]
    for part in parts:
        mixed = mixed + part[...].astype(jnp.float32)
    final = norm_rows(mixed, gain_ref[...])
    projected = jnp.dot(final, proj_ref[...], preferred_element_type=jnp.float32)
    total = jnp.sum(projected * projected, axis=-1, keepdims=True)
    vectors = (projected * lax.rsqrt(total + 1e-06)).astype(jnp.bfloat16)
    vectors_ref[...] = vectors
    group, me = lax.axis_index("group"), lax.axis_index("dev")
    rows = vectors.shape[0]
    docs = out_ref.shape[1]
    spot = me * rows + lax.broadcasted_iota(jnp.int32, (rows, 128), 0)
    inside, low = [], jnp.int32(0)
    for doc in range(docs):
        high = low + lengths_ref[0, doc]
        inside.append((spot >= low) & (spot < high))
        low = high
    for far, block in enumerate(queries):
        for start in range(0, block.shape[0], 128):
            similar = dot_nt(vectors, block[start : start + 128, :])
            best = [
                jnp.max(jnp.where(inside[doc], similar, -jnp.inf), axis=0, keepdims=True)
                for doc in range(docs)
            ]
            best = jnp.concatenate(best, axis=0).astype(jnp.bfloat16)
            target = (group ^ far) * (2 * chips) + start // 64
            out_ref[target] = best
            out_ref[target + 1] = best


def pick_kernel(query_len, cand_ref, best_ref, out_ref):
    groups, _, docs, lanes = best_ref.shape
    own, listed = cand_ref.shape
    offset = (lax.axis_index("dev") % 2) * own * query_len
    scores = [jnp.zeros((1, listed), jnp.float32) for _ in range(own)]
    lane = lax.broadcasted_iota(jnp.int32, (docs, lanes), 1)
    label = lax.broadcasted_iota(jnp.int32, (docs, listed), 0)
    for far in range(groups):
        best = jnp.max(best_ref[far].astype(jnp.float32), axis=0)
        for query in range(own):
            start = offset + query * query_len
            taken = jnp.where((lane >= start) & (lane < start + query_len), best, 0.0)
            value = jnp.sum(taken, axis=1, keepdims=True) / query_len
            wanted = cand_ref[query : query + 1, :] - far * docs
            scores[query] += jnp.sum(jnp.where(wanted == label, value, 0.0), axis=0, keepdims=True)
    for query in range(own):
        out_ref[query : query + 1, :] = scores[query]


def body(
    corpus_tokens,
    norm_gain,
    wi_weight,
    wo_weight,
    final_gain,
    proj_weight,
    query_vectors,
    doc_lengths,
    candidates,
):
    groups = lax.axis_size("group")
    devices = lax.axis_size("dev")
    chips = devices // 2
    rows, width = corpus_tokens.shape
    part = wo_weight.shape[0] * 2
    smem = pl.BlockSpec(memory_space=pltpu.SMEM)
    vmem = pl.BlockSpec(memory_space=pltpu.VMEM)
    params = pltpu.CompilerParams(vmem_limit_bytes=VMEM_LIMIT)

    def swap(values, mask, axis="dev"):
        size = devices if axis == "dev" else groups
        return lax.ppermute(values, axis, [(i, i ^ mask) for i in range(size)])

    per_query, query_len, vector_dim = query_vectors.shape
    query_own = query_vectors.reshape(-1, vector_dim)
    wo_other = swap(wo_weight, 1)
    tokens = [corpus_tokens] + [swap(corpus_tokens, 2 * step) for step in range(1, chips)]
    if wi_weight.shape[0] == 128 and part % 16 == 0:
        piece_shape = jax.ShapeDtypeStruct((2 * part + query_own.shape[0], 128), jnp.bfloat16)
        pieces = pl.pallas_call(
            functools.partial(split_kernel, chips),
            out_shape=[piece_shape] * chips,
            in_specs=[vmem] * 2,
            out_specs=[vmem] * chips,
            scratch_shapes=[pltpu.VMEM((wi_weight.shape[1], 128), jnp.bfloat16)],
            compiler_params=params,
        )(wi_weight, query_own)
        mine = [pieces[0]] + [swap(pieces[step], 2 * step) for step in range(1, chips)]
        mine[1], tokens[1], tokens[2] = lax.optimization_barrier((mine[1], tokens[1], tokens[2]))
        other = [swap(piece, 1) for piece in mine]
        *weights, plane = pl.pallas_call(
            functools.partial(join_kernel, chips),
            out_shape=[
                jax.ShapeDtypeStruct((part, width), jnp.bfloat16),
                jax.ShapeDtypeStruct((part, width), jnp.bfloat16),
                jax.ShapeDtypeStruct((part, wo_weight.shape[1]), jnp.bfloat16),
                jax.ShapeDtypeStruct((devices * query_own.shape[0], vector_dim), jnp.bfloat16),
            ],
            in_specs=[vmem] * (2 + 2 * chips),
            out_specs=[vmem] * 4,
            compiler_params=params,
        )(wo_weight, wo_other, *mine, *other)
    else:
        me = lax.axis_index("dev")
        whole = lax.all_gather(wi_weight, "dev", axis=0, tiled=True).reshape(width, 2, chips, part)
        columns = lax.dynamic_index_in_dim(whole, me // 2, 2, keepdims=False)
        even = (me % 2) == 0
        wo_part = jnp.concatenate(
            [jnp.where(even, wo_weight, wo_other), jnp.where(even, wo_other, wo_weight)], axis=0
        )
        weights = [columns[:, 0].T, columns[:, 1].T, wo_part]
        plane = lax.all_gather(query_own, "dev", axis=0, tiled=True)
    partial = [None] * chips
    for step in list(range(1, chips)) + [0]:
        partial[step] = pl.pallas_call(
            ffn_kernel,
            out_shape=jax.ShapeDtypeStruct((rows, width), jnp.bfloat16 if step else jnp.float32),
            in_specs=[vmem] * 5,
            out_specs=vmem,
            compiler_params=params,
        )(norm_gain.reshape(1, -1), *weights, tokens[step])
    arrived = [swap(partial[step], 2 * step) for step in range(1, chips)]
    queries = [plane] + [swap(plane, mask, "group") for mask in range(1, groups)]

    docs = doc_lengths.shape[1]
    vectors, best = pl.pallas_call(
        functools.partial(finish_kernel, chips),
        out_shape=[
            jax.ShapeDtypeStruct((rows, proj_weight.shape[1]), jnp.bfloat16),
            jax.ShapeDtypeStruct((groups * devices, docs, 128), jnp.bfloat16),
        ],
        in_specs=[smem] + [vmem] * (4 + chips - 1 + groups),
        out_specs=[vmem, vmem],
        compiler_params=params,
    )(
        doc_lengths,
        corpus_tokens,
        final_gain.reshape(1, -1),
        proj_weight,
        partial[0],
        *arrived[::-1],
        *queries,
    )
    met = lax.all_to_all(best, ("group", "dev"), split_axis=0, concat_axis=0, tiled=True)
    scores = pl.pallas_call(
        functools.partial(pick_kernel, query_len),
        out_shape=jax.ShapeDtypeStruct(candidates.shape, jnp.float32),
        in_specs=[vmem, vmem],
        out_specs=vmem,
        compiler_params=params,
    )(candidates, met.reshape(groups, devices, docs, 128))
    return (vectors, scores)


def solution(mesh):
    placed = (
        P(("group", "dev"), None),
        P(),
        P("dev", None),
        P("dev", None),
        P(),
        P(),
        P(("group", "dev"), None, None),
        P("group", None),
        P(("group", "dev"), None),
    )
    return jax.shard_map(
        body,
        mesh=mesh,
        in_specs=placed,
        out_specs=(P(("group", "dev"), None), P(("group", "dev"), None)),
        check_vma=False,
    )
```

```python
import functools

import jax
import jax.numpy as jnp
from jax import lax
from jax.experimental import pallas as pl
from jax.experimental.pallas import tpu as pltpu
from jax.sharding import PartitionSpec as P

VMEM_LIMIT = 20 * 1024 * 1024


def norm_rows(values, gain_row):
    center = jnp.mean(values, axis=-1, keepdims=True)
    shifted = values - center
    spread = jnp.mean(shifted * shifted, axis=-1, keepdims=True)
    return (shifted * lax.rsqrt(spread + 1e-05) * gain_row).astype(jnp.bfloat16)


def dot_nt(left, right):
    return lax.dot_general(
        left, right, (((1,), (1,)), ((), ())), preferred_element_type=jnp.float32
    )


def split_kernel(chips, groups, wi_ref, *refs):
    lines, pieces, turned = refs[:groups], refs[groups:-1], refs[-1]
    columns = wi_ref.shape[1]
    width = columns // 2
    part = width // chips
    chip = lax.axis_index("dev") // 2
    for start in range(0, columns, 128):
        turned[start : start + 128, :] = wi_ref[:, start : start + 128].T
    for step in range(chips):
        for half in range(2):
            first = pl.multiple_of(half * width + (chip ^ step) * part, 16)
            pieces[step][half * part : (half + 1) * part] = turned[pl.ds(first, part), :]
        for far, line in enumerate(lines):
            rows = line.shape[0]
            pieces[step][2 * part + far * rows : 2 * part + (far + 1) * rows] = line[...]


def join_kernel(chips, wo_mine, wo_other, *refs):
    mine, other = refs[:chips], refs[chips : 2 * chips]
    gelu_w, gate_w, wo_part, queries = refs[2 * chips :]
    chip, core = lax.axis_index("dev") // 2, lax.axis_index("dev") % 2
    rows = wo_mine.shape[0]
    for first, upper, lower in ((0, wo_mine, wo_other), (1, wo_other, wo_mine)):

        @pl.when(core == first)
        def _(upper=upper, lower=lower):
            wo_part[:rows] = upper[...]
            wo_part[rows:] = lower[...]

    part = gelu_w.shape[0]
    own = mine[0].shape[0] - 2 * part
    for step in range(chips):
        source = (chip ^ step) * 2
        for block, at in ((mine[step], source + core), (other[step], source + 1 - core)):
            columns = pl.ds(pl.multiple_of(at * 128, 128), 128)
            gelu_w[:, columns] = block[:part]
            gate_w[:, columns] = block[part : 2 * part]
            queries[pl.ds(pl.multiple_of(at * own, own), own), :] = block[2 * part :]


def ffn_kernel(gain_ref, gelu_w, gate_w, wo_part, *refs):
    tokens, out_ref = jnp.concatenate([ref[...] for ref in refs[:-1]], axis=0), refs[-1]
    normed = norm_rows(tokens.astype(jnp.float32), gain_ref[...])
    first = dot_nt(normed, gelu_w[...])
    second = dot_nt(normed, gate_w[...])
    hidden = (0.5 * first * (1.0 + lax.erf(first * 0.7071067811865476)) * second).astype(jnp.bfloat16)
    out_ref[...] = jnp.dot(hidden, wo_part[...], preferred_element_type=jnp.float32).astype(
        out_ref.dtype
    )


def finish_kernel(chips, lengths_ref, tokens_ref, gain_ref, proj_ref, own_ref, *refs):
    parts, refs = refs[: chips - 1], refs[chips - 1 :]
    queries, vectors_ref, out_ref = refs
    mixed = tokens_ref[...].astype(jnp.float32) + own_ref[...]
    for part in parts:
        mixed = mixed + part[...].astype(jnp.float32)
    final = norm_rows(mixed, gain_ref[...])
    projected = jnp.dot(final, proj_ref[...], preferred_element_type=jnp.float32)
    total = jnp.sum(projected * projected, axis=-1, keepdims=True)
    vectors = (projected * lax.rsqrt(total + 1e-06)).astype(jnp.bfloat16)
    vectors_ref[...] = vectors
    group, me = lax.axis_index("group"), lax.axis_index("dev")
    rows = vectors.shape[0]
    docs = out_ref.shape[1]
    devices = 2 * chips
    groups = out_ref.shape[0] // devices
    spot = me * rows + lax.broadcasted_iota(jnp.int32, (rows, 128), 0)
    inside, low = [], jnp.int32(0)
    for doc in range(docs):
        high = low + lengths_ref[0, doc]
        inside.append((spot >= low) & (spot < high))
        low = high
    for start in range(0, queries.shape[0], 128):
        similar = dot_nt(vectors, queries[start : start + 128, :])
        best = [
            jnp.max(jnp.where(inside[doc], similar, -jnp.inf), axis=0, keepdims=True)
            for doc in range(docs)
        ]
        best = jnp.concatenate(best, axis=0).astype(jnp.bfloat16)
        device, far = divmod(start // 64, groups)
        out_ref[(group ^ far) * devices + device] = best
        out_ref[(group ^ (far + 1)) * devices + device] = best


def pick_kernel(query_len, cand_ref, best_ref, out_ref):
    groups, _, docs, lanes = best_ref.shape
    own, listed = cand_ref.shape
    scores = [jnp.zeros((1, listed), jnp.float32) for _ in range(own)]
    lane = lax.broadcasted_iota(jnp.int32, (docs, lanes), 1)
    label = lax.broadcasted_iota(jnp.int32, (docs, listed), 0)
    for far in range(groups):
        best = jnp.max(best_ref[far].astype(jnp.float32), axis=0)
        for query in range(own):
            start = ((lax.axis_index("group") ^ far) % 2) * own * query_len + query * query_len
            taken = jnp.where((lane >= start) & (lane < start + query_len), best, 0.0)
            value = jnp.sum(taken, axis=1, keepdims=True) / query_len
            wanted = cand_ref[query : query + 1, :] - far * docs
            scores[query] += jnp.sum(jnp.where(wanted == label, value, 0.0), axis=0, keepdims=True)
    for query in range(own):
        out_ref[query : query + 1, :] = scores[query]


def body(
    corpus_tokens,
    norm_gain,
    wi_weight,
    wo_weight,
    final_gain,
    proj_weight,
    query_vectors,
    doc_lengths,
    candidates,
):
    groups = lax.axis_size("group")
    devices = lax.axis_size("dev")
    chips = devices // 2
    rows, width = corpus_tokens.shape
    part = wo_weight.shape[0] * 2
    smem = pl.BlockSpec(memory_space=pltpu.SMEM)
    vmem = pl.BlockSpec(memory_space=pltpu.VMEM)
    params = pltpu.CompilerParams(vmem_limit_bytes=VMEM_LIMIT)

    def swap(values, mask, axis="dev"):
        size = devices if axis == "dev" else groups
        return lax.ppermute(values, axis, [(i, i ^ mask) for i in range(size)])

    per_query, query_len, vector_dim = query_vectors.shape
    query_own = query_vectors.reshape(-1, vector_dim)
    lines = [query_own] + [swap(query_own, mask, "group") for mask in range(1, groups)]
    line_rows = groups * query_own.shape[0]
    near = [corpus_tokens] + [swap(corpus_tokens, 2 * step) for step in (1, 2)]
    if wi_weight.shape[0] == 128 and part % 16 == 0 and chips == 4:
        piece_shape = jax.ShapeDtypeStruct((2 * part + line_rows, 128), jnp.bfloat16)
        pieces = pl.pallas_call(
            functools.partial(split_kernel, chips, groups),
            out_shape=[piece_shape] * chips,
            in_specs=[vmem] * (1 + groups),
            out_specs=[vmem] * chips,
            scratch_shapes=[pltpu.VMEM((wi_weight.shape[1], 128), jnp.bfloat16)],
            compiler_params=params,
        )(wi_weight, *lines)
        mine = [pieces[0]] + [swap(pieces[step], 2 * step) for step in range(1, chips)]
        near[1], near[2], wo_own = lax.optimization_barrier((near[1], near[2], wo_weight))
        wo_other = swap(wo_own, 1)
        mine[1], near[1], near[2] = lax.optimization_barrier((mine[1], near[1], near[2]))
        far = [swap(near[2][: rows // 2], 2), swap(near[1][rows // 2 :], 4)]
        tokens = [[each] for each in near] + [far]
        other = [swap(piece, 1) for piece in mine]
        *weights, queries = pl.pallas_call(
            functools.partial(join_kernel, chips),
            out_shape=[
                jax.ShapeDtypeStruct((part, width), jnp.bfloat16),
                jax.ShapeDtypeStruct((part, width), jnp.bfloat16),
                jax.ShapeDtypeStruct((part, wo_weight.shape[1]), jnp.bfloat16),
                jax.ShapeDtypeStruct((devices * line_rows, vector_dim), jnp.bfloat16),
            ],
            in_specs=[vmem] * (2 + 2 * chips),
            out_specs=[vmem] * 4,
            compiler_params=params,
        )(wo_weight, wo_other, *mine, *other)
    else:
        me = lax.axis_index("dev")
        whole = lax.all_gather(wi_weight, "dev", axis=0, tiled=True).reshape(width, 2, chips, part)
        columns = lax.dynamic_index_in_dim(whole, me // 2, 2, keepdims=False)
        even = (me % 2) == 0
        wo_other = swap(wo_weight, 1)
        wo_part = jnp.concatenate(
            [jnp.where(even, wo_weight, wo_other), jnp.where(even, wo_other, wo_weight)], axis=0
        )
        weights = [columns[:, 0].T, columns[:, 1].T, wo_part]
        queries = lax.all_gather(jnp.concatenate(lines, axis=0), "dev", axis=0, tiled=True)
        tokens = [[each] for each in near]
        tokens += [[swap(corpus_tokens, 2 * step)] for step in range(3, chips)]
    partial, arrived = [None] * chips, [None] * chips
    for step in list(range(1, chips)) + [0]:
        if step == 0:
            arrived[1], tokens[0][0] = lax.optimization_barrier((arrived[1], tokens[0][0]))
        partial[step] = pl.pallas_call(
            ffn_kernel,
            out_shape=jax.ShapeDtypeStruct((rows, width), jnp.bfloat16 if step else jnp.float32),
            in_specs=[vmem] * (4 + len(tokens[step])),
            out_specs=vmem,
            compiler_params=params,
        )(norm_gain.reshape(1, -1), *weights, *tokens[step])
        if step:
            arrived[step] = swap(partial[step], 2 * step)

    docs = doc_lengths.shape[1]
    vectors, best = pl.pallas_call(
        functools.partial(finish_kernel, chips),
        out_shape=[
            jax.ShapeDtypeStruct((rows, proj_weight.shape[1]), jnp.bfloat16),
            jax.ShapeDtypeStruct((groups * devices, docs, 128), jnp.bfloat16),
        ],
        in_specs=[smem] + [vmem] * (4 + chips - 1 + 1),
        out_specs=[vmem, vmem],
        compiler_params=params,
    )(
        doc_lengths,
        corpus_tokens,
        final_gain.reshape(1, -1),
        proj_weight,
        partial[0],
        *arrived[:0:-1],
        queries,
    )
    met = lax.all_to_all(best, ("group", "dev"), split_axis=0, concat_axis=0, tiled=True)
    scores = pl.pallas_call(
        functools.partial(pick_kernel, query_len),
        out_shape=jax.ShapeDtypeStruct(candidates.shape, jnp.float32),
        in_specs=[vmem, vmem],
        out_specs=vmem,
        compiler_params=params,
    )(candidates, met.reshape(groups, devices, docs, 128))
    return (vectors, scores)


def solution(mesh):
    placed = (
        P(("group", "dev"), None),
        P(),
        P("dev", None),
        P("dev", None),
        P(),
        P(),
        P(("group", "dev"), None, None),
        P("group", None),
        P(("group", "dev"), None),
    )
    return jax.shard_map(
        body,
        mesh=mesh,
        in_specs=placed,
        out_specs=(P(("group", "dev"), None), P(("group", "dev"), None)),
        check_vma=False,
    )
```

```python
import functools

import jax
import jax.numpy as jnp
from jax import lax
from jax.experimental import pallas as pl
from jax.experimental.pallas import tpu as pltpu
from jax.sharding import PartitionSpec as P

VMEM_LIMIT = 20 * 1024 * 1024


def norm_rows(values, gain_row):
    center = jnp.mean(values, axis=-1, keepdims=True)
    shifted = values - center
    spread = jnp.mean(shifted * shifted, axis=-1, keepdims=True)
    return (shifted * lax.rsqrt(spread + 1e-05) * gain_row).astype(jnp.bfloat16)


def dot_nt(left, right):
    return lax.dot_general(
        left, right, (((1,), (1,)), ((), ())), preferred_element_type=jnp.float32
    )


def split_kernel(chips, wi_ref, query_ref, *refs):
    pieces, turned = refs[:chips], refs[chips]
    columns = wi_ref.shape[1]
    width = columns // 2
    part = width // chips
    chip = lax.axis_index("dev") // 2
    for start in range(0, columns, 128):
        turned[start : start + 128, :] = wi_ref[:, start : start + 128].T
    for step in range(chips):
        halves = (0, 1) if step < 3 else (lax.axis_index("group") % 2,)
        for at, half in enumerate(halves):
            first = pl.multiple_of(half * width + (chip ^ step) * part, 16)
            pieces[step][at * part : (at + 1) * part] = turned[pl.ds(first, part), :]
        pieces[step][len(halves) * part :] = query_ref[...]


def join_kernel(chips, wo_mine, wo_other, *refs):
    mine, other = refs[: chips + 1], refs[chips + 1 : 2 * chips + 2]
    gelu_w, gate_w, wo_part, queries = refs[2 * chips + 2 :]
    chip, core = lax.axis_index("dev") // 2, lax.axis_index("dev") % 2
    rows = wo_mine.shape[0]
    for first, upper, lower in ((0, wo_mine, wo_other), (1, wo_other, wo_mine)):

        @pl.when(core == first)
        def _(upper=upper, lower=lower):
            wo_part[:rows] = upper[...]
            wo_part[rows:] = lower[...]

    part = gelu_w.shape[0]
    own = mine[0].shape[0] - 2 * part
    for step in range(chips):
        source = (chip ^ step) * 2
        for blocks, at in ((mine, source + core), (other, source + 1 - core)):
            columns = pl.ds(pl.multiple_of(at * 128, 128), 128)
            if step < 3:
                gelu_w[:, columns] = blocks[step][:part]
                gate_w[:, columns] = blocks[step][part : 2 * part]
            else:
                for parity in range(2):

                    @pl.when(lax.axis_index("group") % 2 == parity)
                    def _(parity=parity, blocks=blocks, columns=columns):
                        gelu_w[:, columns] = blocks[3 + parity][:part]
                        gate_w[:, columns] = blocks[4 - parity][:part]

            last = 2 * part if step < 3 else part
            queries[pl.ds(pl.multiple_of(at * own, own), own), :] = blocks[step][last : last + own]


def ffn_kernel(gain_ref, gelu_w, gate_w, wo_part, *refs):
    tokens, out_ref = jnp.concatenate([ref[...] for ref in refs[:-1]], axis=0), refs[-1]
    normed = norm_rows(tokens.astype(jnp.float32), gain_ref[...])
    first = dot_nt(normed, gelu_w[...])
    second = dot_nt(normed, gate_w[...])
    hidden = (0.5 * first * (1.0 + lax.erf(first * 0.7071067811865476)) * second).astype(jnp.bfloat16)
    out_ref[...] = jnp.dot(hidden, wo_part[...], preferred_element_type=jnp.float32).astype(
        out_ref.dtype
    )


def finish_kernel(chips, lengths_ref, tokens_ref, gain_ref, proj_ref, own_ref, *refs):
    parts, refs = refs[: chips - 1], refs[chips - 1 :]
    queries, (vectors_ref, out_ref) = refs[:-2], refs[-2:]
    mixed = tokens_ref[...].astype(jnp.float32) + own_ref[...]
    for part in parts:
        mixed = mixed + part[...].astype(jnp.float32)
    final = norm_rows(mixed, gain_ref[...])
    projected = jnp.dot(final, proj_ref[...], preferred_element_type=jnp.float32)
    total = jnp.sum(projected * projected, axis=-1, keepdims=True)
    vectors = (projected * lax.rsqrt(total + 1e-06)).astype(jnp.bfloat16)
    vectors_ref[...] = vectors
    group, me = lax.axis_index("group"), lax.axis_index("dev")
    rows = vectors.shape[0]
    docs = out_ref.shape[1]
    spot = me * rows + lax.broadcasted_iota(jnp.int32, (rows, 128), 0)
    inside, low = [], jnp.int32(0)
    for doc in range(docs):
        high = low + lengths_ref[0, doc]
        inside.append((spot >= low) & (spot < high))
        low = high
    for far, block in enumerate(queries):
        for start in range(0, block.shape[0], 128):
            similar = dot_nt(vectors, block[start : start + 128, :])
            best = [
                jnp.max(jnp.where(inside[doc], similar, -jnp.inf), axis=0, keepdims=True)
                for doc in range(docs)
            ]
            best = jnp.concatenate(best, axis=0).astype(jnp.bfloat16)
            target = (group ^ far) * (2 * chips) + start // 64
            out_ref[target] = best
            out_ref[target + 1] = best


def pick_kernel(query_len, cand_ref, best_ref, out_ref):
    groups, _, docs, lanes = best_ref.shape
    own, listed = cand_ref.shape
    offset = (lax.axis_index("dev") % 2) * own * query_len
    scores = [jnp.zeros((1, listed), jnp.float32) for _ in range(own)]
    lane = lax.broadcasted_iota(jnp.int32, (docs, lanes), 1)
    label = lax.broadcasted_iota(jnp.int32, (docs, listed), 0)
    for far in range(groups):
        best = jnp.max(best_ref[far].astype(jnp.float32), axis=0)
        for query in range(own):
            start = offset + query * query_len
            taken = jnp.where((lane >= start) & (lane < start + query_len), best, 0.0)
            value = jnp.sum(taken, axis=1, keepdims=True) / query_len
            wanted = cand_ref[query : query + 1, :] - far * docs
            scores[query] += jnp.sum(jnp.where(wanted == label, value, 0.0), axis=0, keepdims=True)
    for query in range(own):
        out_ref[query : query + 1, :] = scores[query]


def body(
    corpus_tokens,
    norm_gain,
    wi_weight,
    wo_weight,
    final_gain,
    proj_weight,
    query_vectors,
    doc_lengths,
    candidates,
):
    groups = lax.axis_size("group")
    devices = lax.axis_size("dev")
    chips = devices // 2
    rows, width = corpus_tokens.shape
    part = wo_weight.shape[0] * 2
    smem = pl.BlockSpec(memory_space=pltpu.SMEM)
    vmem = pl.BlockSpec(memory_space=pltpu.VMEM)
    params = pltpu.CompilerParams(vmem_limit_bytes=VMEM_LIMIT)

    def swap(values, mask, axis="dev"):
        size = devices if axis == "dev" else groups
        return lax.ppermute(values, axis, [(i, i ^ mask) for i in range(size)])

    per_query, query_len, vector_dim = query_vectors.shape
    query_own = query_vectors.reshape(-1, vector_dim)
    wo_other = swap(wo_weight, 1)
    near = [corpus_tokens] + [swap(corpus_tokens, 2 * step) for step in (1, 2)]
    if wi_weight.shape[0] == 128 and part % 16 == 0 and chips == 4 and groups % 2 == 0:
        own = query_own.shape[0]
        pieces = pl.pallas_call(
            functools.partial(split_kernel, chips),
            out_shape=[
                jax.ShapeDtypeStruct(((2 if step < 3 else 1) * part + own, 128), jnp.bfloat16)
                for step in range(chips)
            ],
            in_specs=[vmem] * 2,
            out_specs=[vmem] * chips,
            scratch_shapes=[pltpu.VMEM((wi_weight.shape[1], 128), jnp.bfloat16)],
            compiler_params=params,
        )(wi_weight, query_own)
        mine = [pieces[0]] + [swap(pieces[step], 2 * step) for step in range(1, chips)]
        mine.append(swap(mine[3], 1, "group"))
        mine[1], near[1], near[2] = lax.optimization_barrier((mine[1], near[1], near[2]))
        far = [swap(near[2][: rows // 2], 2), swap(near[1][rows // 2 :], 4)]
        tokens = [[each] for each in near] + [far]
        other = [swap(piece, 1) for piece in mine]
        *weights, plane = pl.pallas_call(
            functools.partial(join_kernel, chips),
            out_shape=[
                jax.ShapeDtypeStruct((part, width), jnp.bfloat16),
                jax.ShapeDtypeStruct((part, width), jnp.bfloat16),
                jax.ShapeDtypeStruct((part, wo_weight.shape[1]), jnp.bfloat16),
                jax.ShapeDtypeStruct((devices * own, vector_dim), jnp.bfloat16),
            ],
            in_specs=[vmem] * (4 + 2 * chips),
            out_specs=[vmem] * 4,
            compiler_params=params,
        )(wo_weight, wo_other, *mine, *other)
    else:
        me = lax.axis_index("dev")
        whole = lax.all_gather(wi_weight, "dev", axis=0, tiled=True).reshape(width, 2, chips, part)
        columns = lax.dynamic_index_in_dim(whole, me // 2, 2, keepdims=False)
        even = (me % 2) == 0
        wo_part = jnp.concatenate(
            [jnp.where(even, wo_weight, wo_other), jnp.where(even, wo_other, wo_weight)], axis=0
        )
        weights = [columns[:, 0].T, columns[:, 1].T, wo_part]
        tokens = [[each] for each in near]
        tokens += [[swap(corpus_tokens, 2 * step)] for step in range(3, chips)]
        plane = lax.all_gather(query_own, "dev", axis=0, tiled=True)
    partial, arrived = [None] * chips, [None] * chips
    for step in list(range(1, chips)) + [0]:
        if step == 0:
            arrived[1], tokens[0][0] = lax.optimization_barrier((arrived[1], tokens[0][0]))
        partial[step] = pl.pallas_call(
            ffn_kernel,
            out_shape=jax.ShapeDtypeStruct((rows, width), jnp.bfloat16 if step else jnp.float32),
            in_specs=[vmem] * (4 + len(tokens[step])),
            out_specs=vmem,
            compiler_params=params,
        )(norm_gain.reshape(1, -1), *weights, *tokens[step])
        if step:
            arrived[step] = swap(partial[step], 2 * step)
    queries = [plane] + [swap(plane, mask, "group") for mask in range(1, groups)]

    docs = doc_lengths.shape[1]
    vectors, best = pl.pallas_call(
        functools.partial(finish_kernel, chips),
        out_shape=[
            jax.ShapeDtypeStruct((rows, proj_weight.shape[1]), jnp.bfloat16),
            jax.ShapeDtypeStruct((groups * devices, docs, 128), jnp.bfloat16),
        ],
        in_specs=[smem] + [vmem] * (4 + chips - 1 + groups),
        out_specs=[vmem, vmem],
        compiler_params=params,
    )(
        doc_lengths,
        corpus_tokens,
        final_gain.reshape(1, -1),
        proj_weight,
        partial[0],
        *arrived[:0:-1],
        *queries,
    )
    met = lax.all_to_all(best, ("group", "dev"), split_axis=0, concat_axis=0, tiled=True)
    scores = pl.pallas_call(
        functools.partial(pick_kernel, query_len),
        out_shape=jax.ShapeDtypeStruct(candidates.shape, jnp.float32),
        in_specs=[vmem, vmem],
        out_specs=vmem,
        compiler_params=params,
    )(candidates, met.reshape(groups, devices, docs, 128))
    return (vectors, scores)


def solution(mesh):
    placed = (
        P(("group", "dev"), None),
        P(),
        P("dev", None),
        P("dev", None),
        P(),
        P(),
        P(("group", "dev"), None, None),
        P("group", None),
        P(("group", "dev"), None),
    )
    return jax.shard_map(
        body,
        mesh=mesh,
        in_specs=placed,
        out_specs=(P(("group", "dev"), None), P(("group", "dev"), None)),
        check_vma=False,
    )
```

```python
import functools

import jax
import jax.numpy as jnp
from jax import lax
from jax.experimental import pallas as pl
from jax.experimental.pallas import tpu as pltpu
from jax.sharding import PartitionSpec as P

VMEM_LIMIT = 20 * 1024 * 1024


def norm_rows(values, gain_row):
    center = jnp.mean(values, axis=-1, keepdims=True)
    shifted = values - center
    spread = jnp.mean(shifted * shifted, axis=-1, keepdims=True)
    return (shifted * lax.rsqrt(spread + 1e-05) * gain_row).astype(jnp.bfloat16)


def dot_nt(left, right):
    return lax.dot_general(
        left, right, (((1,), (1,)), ((), ())), preferred_element_type=jnp.float32
    )


def split_kernel(chips, wi_ref, query_ref, *refs):
    pieces, turned = refs[:chips], refs[chips]
    columns = wi_ref.shape[1]
    width = columns // 2
    part = width // chips
    chip = lax.axis_index("dev") // 2
    for start in range(0, columns, 128):
        turned[start : start + 128, :] = wi_ref[:, start : start + 128].T
    for step in range(chips):
        halves = (0, 1) if step < 3 else (lax.axis_index("group") % 2,)
        for at, half in enumerate(halves):
            first = pl.multiple_of(half * width + (chip ^ step) * part, 16)
            pieces[step][at * part : (at + 1) * part] = turned[pl.ds(first, part), :]
        if step == 3:
            pieces[step][part:] = query_ref[...]


def stack_kernel(count, *refs):
    rows = refs[0].shape[0]
    for at in range(count):
        refs[count][at * rows : (at + 1) * rows] = refs[at][...]


def join_kernel(chips, wo_mine, wo_other, *refs):
    mine, other = refs[: chips + 1], refs[chips + 1 : 2 * chips + 2]
    gelu_w, gate_w, wo_part = refs[2 * chips + 2 :]
    chip, core = lax.axis_index("dev") // 2, lax.axis_index("dev") % 2
    rows = wo_mine.shape[0]
    for first, upper, lower in ((0, wo_mine, wo_other), (1, wo_other, wo_mine)):

        @pl.when(core == first)
        def _(upper=upper, lower=lower):
            wo_part[:rows] = upper[...]
            wo_part[rows:] = lower[...]

    part = gelu_w.shape[0]
    for step in range(chips):
        source = (chip ^ step) * 2
        for blocks, at in ((mine, source + core), (other, source + 1 - core)):
            columns = pl.ds(pl.multiple_of(at * 128, 128), 128)
            if step < 3:
                gelu_w[:, columns] = blocks[step][:part]
                gate_w[:, columns] = blocks[step][part : 2 * part]
            else:
                for parity in range(2):

                    @pl.when(lax.axis_index("group") % 2 == parity)
                    def _(parity=parity, blocks=blocks, columns=columns):
                        gelu_w[:, columns] = blocks[3 + parity][:part]
                        gate_w[:, columns] = blocks[4 - parity][:part]


def ffn_kernel(gain_ref, gelu_w, gate_w, wo_part, *refs):
    tokens, out_ref = jnp.concatenate([ref[...] for ref in refs[:-1]], axis=0), refs[-1]
    normed = norm_rows(tokens.astype(jnp.float32), gain_ref[...])
    first = dot_nt(normed, gelu_w[...])
    second = dot_nt(normed, gate_w[...])
    hidden = (0.5 * first * (1.0 + lax.erf(first * 0.7071067811865476)) * second).astype(jnp.bfloat16)
    out_ref[...] = jnp.dot(hidden, wo_part[...], preferred_element_type=jnp.float32).astype(
        out_ref.dtype
    )


def finish_kernel(chips, lengths_ref, tokens_ref, gain_ref, proj_ref, own_ref, *refs):
    parts, refs = refs[: chips - 1], refs[chips - 1 :]
    queries, (vectors_ref, out_ref) = refs[:-2], refs[-2:]
    mixed = tokens_ref[...].astype(jnp.float32) + own_ref[...]
    for part in parts:
        mixed = mixed + part[...].astype(jnp.float32)
    final = norm_rows(mixed, gain_ref[...])
    projected = jnp.dot(final, proj_ref[...], preferred_element_type=jnp.float32)
    total = jnp.sum(projected * projected, axis=-1, keepdims=True)
    vectors = (projected * lax.rsqrt(total + 1e-06)).astype(jnp.bfloat16)
    vectors_ref[...] = vectors
    group, me = lax.axis_index("group"), lax.axis_index("dev")
    rows = vectors.shape[0]
    docs = out_ref.shape[1]
    spot = me * rows + lax.broadcasted_iota(jnp.int32, (rows, 128), 0)
    inside, low = [], jnp.int32(0)
    for doc in range(docs):
        high = low + lengths_ref[0, doc]
        inside.append((spot >= low) & (spot < high))
        low = high
    chip, core = me // 2, me % 2
    for side, block in enumerate(queries):
        for pair in range(block.shape[0] // 128):
            similar = dot_nt(vectors, block[pair * 128 : (pair + 1) * 128, :])
            best = [
                jnp.max(jnp.where(inside[doc], similar, -jnp.inf), axis=0, keepdims=True)
                for doc in range(docs)
            ]
            best = jnp.concatenate(best, axis=0).astype(jnp.bfloat16)
            for row in (2 * pair, 2 * pair + 1):
                far, mask = row // chips, row % chips
                out_ref[(group ^ far) * (2 * chips) + (chip ^ mask) * 2 + (core ^ side)] = best


def pick_kernel(query_len, cand_ref, best_ref, out_ref):
    groups, devices, docs, lanes = best_ref.shape
    own, listed = cand_ref.shape
    scores = [jnp.zeros((1, listed), jnp.float32) for _ in range(own)]
    lane = lax.broadcasted_iota(jnp.int32, (docs, lanes // 2), 1)
    label = lax.broadcasted_iota(jnp.int32, (docs, listed), 0)
    for far in range(groups):
        low = best_ref[far, 0].astype(jnp.float32)
        high = best_ref[far, 2].astype(jnp.float32)
        for sender in range(1, devices):
            if sender // 2 % 2:
                high = jnp.maximum(high, best_ref[far, sender].astype(jnp.float32))
            else:
                low = jnp.maximum(low, best_ref[far, sender].astype(jnp.float32))
        odd = lax.axis_index("dev") // 2 % 2
        same = jnp.where(odd == 0, low, high)
        cross = jnp.where(odd == 0, high, low)
        best = jnp.maximum(same[:, : lanes // 2], cross[:, lanes // 2 :])
        for query in range(own):
            start = query * query_len
            taken = jnp.where((lane >= start) & (lane < start + query_len), best, 0.0)
            value = jnp.sum(taken, axis=1, keepdims=True) / query_len
            wanted = cand_ref[query : query + 1, :] - far * docs
            scores[query] += jnp.sum(jnp.where(wanted == label, value, 0.0), axis=0, keepdims=True)
    for query in range(own):
        out_ref[query : query + 1, :] = scores[query]


def body(
    corpus_tokens,
    norm_gain,
    wi_weight,
    wo_weight,
    final_gain,
    proj_weight,
    query_vectors,
    doc_lengths,
    candidates,
):
    groups = lax.axis_size("group")
    devices = lax.axis_size("dev")
    chips = devices // 2
    rows, width = corpus_tokens.shape
    part = wo_weight.shape[0] * 2
    smem = pl.BlockSpec(memory_space=pltpu.SMEM)
    vmem = pl.BlockSpec(memory_space=pltpu.VMEM)
    params = pltpu.CompilerParams(vmem_limit_bytes=VMEM_LIMIT)

    def swap(values, mask, axis="dev"):
        size = devices if axis == "dev" else groups
        return lax.ppermute(values, axis, [(i, i ^ mask) for i in range(size)])

    per_query, query_len, vector_dim = query_vectors.shape
    query_own = query_vectors.reshape(-1, vector_dim)
    def stack(parts):
        shape = (len(parts) * parts[0].shape[0], parts[0].shape[1])
        return pl.pallas_call(
            functools.partial(stack_kernel, len(parts)),
            out_shape=jax.ShapeDtypeStruct(shape, parts[0].dtype),
            in_specs=[vmem] * len(parts),
            out_specs=vmem,
            compiler_params=params,
        )(*parts)

    near = [corpus_tokens] + [swap(corpus_tokens, 2 * step) for step in (1, 2)]
    if wi_weight.shape[0] == 128 and part % 16 == 0 and chips == 4 and groups % 2 == 0:
        own = query_own.shape[0]
        pieces = pl.pallas_call(
            functools.partial(split_kernel, chips),
            out_shape=[
                jax.ShapeDtypeStruct((2 * part if step < 3 else part + own, 128), jnp.bfloat16)
                for step in range(chips)
            ],
            in_specs=[vmem] * 2,
            out_specs=[vmem] * chips,
            scratch_shapes=[pltpu.VMEM((wi_weight.shape[1], 128), jnp.bfloat16)],
            compiler_params=params,
        )(wi_weight, query_own)
        mine = [pieces[0]] + [swap(pieces[step], 2 * step) for step in range(1, chips)]
        mine.append(swap(mine[3], 1, "group"))
        mine[3], query_next = lax.optimization_barrier((mine[3], query_own))
        plane = stack([query_own, swap(query_next, 2), swap(query_next, 4), mine[3][part:]])
        mine[1], mine[4], near[1], near[2], plane = lax.optimization_barrier(
            (mine[1], mine[4], near[1], near[2], plane)
        )
        near[1], near[2], wo_next = lax.optimization_barrier((near[1], near[2], wo_weight))
        wo_other = swap(wo_next, 1)
        lines = [plane] + [swap(plane, mask, "group") for mask in range(1, groups)]
        mine[2], *lines = lax.optimization_barrier((mine[2], *lines))
        far = [swap(near[2][: rows // 2], 2), swap(near[1][rows // 2 :], 4)]
        tokens = [[each] for each in near] + [far]
        other = [swap(piece, 1) for piece in mine]
        weights = pl.pallas_call(
            functools.partial(join_kernel, chips),
            out_shape=[
                jax.ShapeDtypeStruct((part, width), jnp.bfloat16),
                jax.ShapeDtypeStruct((part, width), jnp.bfloat16),
                jax.ShapeDtypeStruct((part, wo_weight.shape[1]), jnp.bfloat16),
            ],
            in_specs=[vmem] * (4 + 2 * chips),
            out_specs=[vmem] * 3,
            compiler_params=params,
        )(wo_weight, wo_other, *mine, *other)
    else:
        me = lax.axis_index("dev")
        whole = lax.all_gather(wi_weight, "dev", axis=0, tiled=True).reshape(width, 2, chips, part)
        columns = lax.dynamic_index_in_dim(whole, me // 2, 2, keepdims=False)
        even = (me % 2) == 0
        wo_other = swap(wo_weight, 1)
        wo_part = jnp.concatenate(
            [jnp.where(even, wo_weight, wo_other), jnp.where(even, wo_other, wo_weight)], axis=0
        )
        weights = [columns[:, 0].T, columns[:, 1].T, wo_part]
        tokens = [[each] for each in near]
        tokens += [[swap(corpus_tokens, 2 * step)] for step in range(3, chips)]
        plane = stack([query_own] + [swap(query_own, 2 * step) for step in range(1, chips)])
        lines = [plane] + [swap(plane, mask, "group") for mask in range(1, groups)]
    partial, arrived = [None] * chips, [None] * chips
    for step in list(range(1, chips)) + [0]:
        if step == 0:
            arrived[1], arrived[2], tokens[0][0] = lax.optimization_barrier(
                (arrived[1], arrived[2], tokens[0][0])
            )
        partial[step] = pl.pallas_call(
            ffn_kernel,
            out_shape=jax.ShapeDtypeStruct((rows, width), jnp.bfloat16 if step else jnp.float32),
            in_specs=[vmem] * (4 + len(tokens[step])),
            out_specs=vmem,
            compiler_params=params,
        )(norm_gain.reshape(1, -1), *weights, *tokens[step])
        if step:
            arrived[step] = swap(partial[step], 2 * step)
    line = stack(lines)
    queries = [line, swap(line, 1)]

    docs = doc_lengths.shape[1]
    vectors, best = pl.pallas_call(
        functools.partial(finish_kernel, chips),
        out_shape=[
            jax.ShapeDtypeStruct((rows, proj_weight.shape[1]), jnp.bfloat16),
            jax.ShapeDtypeStruct((groups * devices, docs, 128), jnp.bfloat16),
        ],
        in_specs=[smem] + [vmem] * (4 + chips - 1 + 2),
        out_specs=[vmem, vmem],
        compiler_params=params,
    )(
        doc_lengths,
        corpus_tokens,
        final_gain.reshape(1, -1),
        proj_weight,
        partial[0],
        *arrived[:0:-1],
        *queries,
    )
    met = lax.all_to_all(best, ("group", "dev"), split_axis=0, concat_axis=0, tiled=True)
    scores = pl.pallas_call(
        functools.partial(pick_kernel, query_len),
        out_shape=jax.ShapeDtypeStruct(candidates.shape, jnp.float32),
        in_specs=[vmem, vmem],
        out_specs=vmem,
        compiler_params=params,
    )(candidates, met.reshape(groups, devices, docs, 128))
    return (vectors, scores)


def solution(mesh):
    placed = (
        P(("group", "dev"), None),
        P(),
        P("dev", None),
        P("dev", None),
        P(),
        P(),
        P(("group", "dev"), None, None),
        P("group", None),
        P(("group", "dev"), None),
    )
    return jax.shard_map(
        body,
        mesh=mesh,
        in_specs=placed,
        out_specs=(P(("group", "dev"), None), P(("group", "dev"), None)),
        check_vma=False,
    )
```

```python
import functools

import jax
import jax.numpy as jnp
from jax import lax
from jax.experimental import pallas as pl
from jax.experimental.pallas import tpu as pltpu
from jax.sharding import PartitionSpec as P

VMEM_LIMIT = 20 * 1024 * 1024


def norm_rows(values, gain_row):
    center = jnp.mean(values, axis=-1, keepdims=True)
    shifted = values - center
    spread = jnp.mean(shifted * shifted, axis=-1, keepdims=True)
    return (shifted * lax.rsqrt(spread + 1e-05) * gain_row).astype(jnp.bfloat16)


def dot_nt(left, right):
    return lax.dot_general(
        left, right, (((1,), (1,)), ((), ())), preferred_element_type=jnp.float32
    )


def split_kernel(chips, wi_ref, query_ref, *refs):
    pieces, turned = refs[:chips], refs[chips]
    columns = wi_ref.shape[1]
    width = columns // 2
    part = width // chips
    chip = lax.axis_index("dev") // 2
    for start in range(0, columns, 128):
        turned[start : start + 128, :] = wi_ref[:, start : start + 128].T
    for step in range(chips):
        halves = (0, 1) if step < 3 else (lax.axis_index("group") % 2,)
        for at, half in enumerate(halves):
            first = pl.multiple_of(half * width + (chip ^ step) * part, 16)
            pieces[step][at * part : (at + 1) * part] = turned[pl.ds(first, part), :]
        pieces[step][len(halves) * part :] = query_ref[...]


def join_kernel(chips, wo_mine, wo_other, *refs):
    mine, other = refs[: chips + 1], refs[chips + 1 : 2 * chips + 2]
    gelu_w, gate_w, wo_part, queries = refs[2 * chips + 2 :]
    chip, core = lax.axis_index("dev") // 2, lax.axis_index("dev") % 2
    rows = wo_mine.shape[0]
    for first, upper, lower in ((0, wo_mine, wo_other), (1, wo_other, wo_mine)):

        @pl.when(core == first)
        def _(upper=upper, lower=lower):
            wo_part[:rows] = upper[...]
            wo_part[rows:] = lower[...]

    part = gelu_w.shape[0]
    own = mine[0].shape[0] - 2 * part
    for step in range(chips):
        source = (chip ^ step) * 2
        for blocks, at in ((mine, source + core), (other, source + 1 - core)):
            columns = pl.ds(pl.multiple_of(at * 128, 128), 128)
            if step < 3:
                gelu_w[:, columns] = blocks[step][:part]
                gate_w[:, columns] = blocks[step][part : 2 * part]
            else:
                for parity in range(2):

                    @pl.when(lax.axis_index("group") % 2 == parity)
                    def _(parity=parity, blocks=blocks, columns=columns):
                        gelu_w[:, columns] = blocks[3 + parity][:part]
                        gate_w[:, columns] = blocks[4 - parity][:part]

            last = 2 * part if step < 3 else part
            queries[pl.ds(pl.multiple_of(at * own, own), own), :] = blocks[step][last : last + own]


def ffn_kernel(gain_ref, gelu_w, gate_w, wo_part, *refs):
    tokens, out_ref = jnp.concatenate([ref[...] for ref in refs[:-1]], axis=0), refs[-1]
    normed = norm_rows(tokens.astype(jnp.float32), gain_ref[...])
    first = dot_nt(normed, gelu_w[...])
    second = dot_nt(normed, gate_w[...])
    hidden = (0.5 * first * (1.0 + lax.erf(first * 0.7071067811865476)) * second).astype(jnp.bfloat16)
    out_ref[...] = jnp.dot(hidden, wo_part[...], preferred_element_type=jnp.float32).astype(
        out_ref.dtype
    )


def finish_kernel(chips, lengths_ref, tokens_ref, gain_ref, proj_ref, own_ref, *refs):
    parts, (vectors_ref, sent_ref) = refs[: chips - 1], refs[chips - 1 :]
    mixed = tokens_ref[...].astype(jnp.float32) + own_ref[...]
    for part in parts:
        mixed = mixed + part[...].astype(jnp.float32)
    final = norm_rows(mixed, gain_ref[...])
    projected = jnp.dot(final, proj_ref[...], preferred_element_type=jnp.float32)
    total = jnp.sum(projected * projected, axis=-1, keepdims=True)
    vectors = (projected * lax.rsqrt(total + 1e-06)).astype(jnp.bfloat16)
    vectors_ref[...] = vectors
    rows = vectors.shape[0]
    sent_ref[:rows] = vectors
    spot = lax.axis_index("dev") * rows + lax.broadcasted_iota(jnp.int32, (16, rows), 1)
    owner, end = jnp.zeros((16, rows), jnp.float32), jnp.int32(0)
    for doc in range(lengths_ref.shape[1]):
        end = end + lengths_ref[0, doc]
        owner = owner + (spot >= end).astype(jnp.float32)
    sent_ref[rows:] = owner.astype(jnp.bfloat16)


def score_kernel(groups, query_ref, *refs):
    blocks, out_ref = refs[:groups], refs[groups]
    group = lax.axis_index("group")
    docs = out_ref.shape[2]
    rows = query_ref.shape[1]
    for far, block in enumerate(blocks):
        vectors = block[:rows]
        owner = jnp.broadcast_to(block[rows : rows + 1].astype(jnp.float32), (rows, rows)).T
        for tile in range(query_ref.shape[0] // 128):
            similar = dot_nt(vectors, query_ref[tile * 128 : (tile + 1) * 128, :])
            best = [
                jnp.max(jnp.where(owner == doc, similar, -jnp.inf), axis=0, keepdims=True)
                for doc in range(docs)
            ]
            best = jnp.concatenate(best, axis=0).astype(jnp.bfloat16)
            out_ref[2 * tile, group ^ far] = best
            out_ref[2 * tile + 1, group ^ far] = best


def pick_kernel(query_len, cand_ref, best_ref, out_ref):
    devices, groups, docs, lanes = best_ref.shape
    own, listed = cand_ref.shape
    offset = (lax.axis_index("dev") % 2) * own * query_len
    scores = [jnp.zeros((1, listed), jnp.float32) for _ in range(own)]
    lane = lax.broadcasted_iota(jnp.int32, (docs, lanes), 1)
    label = lax.broadcasted_iota(jnp.int32, (docs, listed), 0)
    for group in range(groups):
        best = best_ref[0, group].astype(jnp.float32)
        for sender in range(1, devices):
            best = jnp.maximum(best, best_ref[sender, group].astype(jnp.float32))
        for query in range(own):
            start = offset + query * query_len
            taken = jnp.where((lane >= start) & (lane < start + query_len), best, 0.0)
            value = jnp.sum(taken, axis=1, keepdims=True) / query_len
            wanted = cand_ref[query : query + 1, :] - group * docs
            scores[query] += jnp.sum(jnp.where(wanted == label, value, 0.0), axis=0, keepdims=True)
    for query in range(own):
        out_ref[query : query + 1, :] = scores[query]


def body(
    corpus_tokens,
    norm_gain,
    wi_weight,
    wo_weight,
    final_gain,
    proj_weight,
    query_vectors,
    doc_lengths,
    candidates,
):
    groups = lax.axis_size("group")
    devices = lax.axis_size("dev")
    chips = devices // 2
    rows, width = corpus_tokens.shape
    part = wo_weight.shape[0] * 2
    smem = pl.BlockSpec(memory_space=pltpu.SMEM)
    vmem = pl.BlockSpec(memory_space=pltpu.VMEM)
    params = pltpu.CompilerParams(vmem_limit_bytes=VMEM_LIMIT)

    def swap(values, mask, axis="dev"):
        size = devices if axis == "dev" else groups
        return lax.ppermute(values, axis, [(i, i ^ mask) for i in range(size)])

    per_query, query_len, vector_dim = query_vectors.shape
    query_own = query_vectors.reshape(-1, vector_dim)
    near = [corpus_tokens] + [swap(corpus_tokens, 2 * step) for step in (1, 2)]
    if wi_weight.shape[0] == 128 and part % 16 == 0 and chips == 4 and groups % 2 == 0:
        own = query_own.shape[0]
        pieces = pl.pallas_call(
            functools.partial(split_kernel, chips),
            out_shape=[
                jax.ShapeDtypeStruct(((2 if step < 3 else 1) * part + own, 128), jnp.bfloat16)
                for step in range(chips)
            ],
            in_specs=[vmem] * 2,
            out_specs=[vmem] * chips,
            scratch_shapes=[pltpu.VMEM((wi_weight.shape[1], 128), jnp.bfloat16)],
            compiler_params=params,
        )(wi_weight, query_own)
        mine = [pieces[0]] + [swap(pieces[step], 2 * step) for step in range(1, chips)]
        mine.append(swap(mine[3], 1, "group"))
        mine[1], mine[4], near[1], near[2] = lax.optimization_barrier((mine[1], mine[4], near[1], near[2]))
        near[1], near[2], wo_next = lax.optimization_barrier((near[1], near[2], wo_weight))
        wo_other = swap(wo_next, 1)
        far = [swap(near[2][: rows // 2], 2), swap(near[1][rows // 2 :], 4)]
        tokens = [[each] for each in near] + [far]
        other = [swap(piece, 1) for piece in mine]
        *weights, plane = pl.pallas_call(
            functools.partial(join_kernel, chips),
            out_shape=[
                jax.ShapeDtypeStruct((part, width), jnp.bfloat16),
                jax.ShapeDtypeStruct((part, width), jnp.bfloat16),
                jax.ShapeDtypeStruct((part, wo_weight.shape[1]), jnp.bfloat16),
                jax.ShapeDtypeStruct((devices * own, vector_dim), jnp.bfloat16),
            ],
            in_specs=[vmem] * (4 + 2 * chips),
            out_specs=[vmem] * 4,
            compiler_params=params,
        )(wo_weight, wo_other, *mine, *other)
    else:
        me = lax.axis_index("dev")
        whole = lax.all_gather(wi_weight, "dev", axis=0, tiled=True).reshape(width, 2, chips, part)
        columns = lax.dynamic_index_in_dim(whole, me // 2, 2, keepdims=False)
        even = (me % 2) == 0
        wo_other = swap(wo_weight, 1)
        wo_part = jnp.concatenate(
            [jnp.where(even, wo_weight, wo_other), jnp.where(even, wo_other, wo_weight)], axis=0
        )
        weights = [columns[:, 0].T, columns[:, 1].T, wo_part]
        tokens = [[each] for each in near]
        tokens += [[swap(corpus_tokens, 2 * step)] for step in range(3, chips)]
        plane = lax.all_gather(query_own, "dev", axis=0, tiled=True)
    partial, arrived = [None] * chips, [None] * chips
    for step in list(range(1, chips)) + [0]:
        if step == 0:
            arrived[1], tokens[0][0] = lax.optimization_barrier((arrived[1], tokens[0][0]))
        partial[step] = pl.pallas_call(
            ffn_kernel,
            out_shape=jax.ShapeDtypeStruct((rows, width), jnp.bfloat16 if step else jnp.float32),
            in_specs=[vmem] * (4 + len(tokens[step])),
            out_specs=vmem,
            compiler_params=params,
        )(norm_gain.reshape(1, -1), *weights, *tokens[step])
        if step:
            arrived[step] = swap(partial[step], 2 * step)

    vectors, sent = pl.pallas_call(
        functools.partial(finish_kernel, chips),
        out_shape=[
            jax.ShapeDtypeStruct((rows, vector_dim), jnp.bfloat16),
            jax.ShapeDtypeStruct((rows + 16, vector_dim), jnp.bfloat16),
        ],
        in_specs=[smem] + [vmem] * (4 + chips - 1),
        out_specs=[vmem, vmem],
        compiler_params=params,
    )(
        doc_lengths,
        corpus_tokens,
        final_gain.reshape(1, -1),
        proj_weight,
        partial[0],
        *arrived[:0:-1],
    )
    blocks = [sent] + [swap(sent, mask, "group") for mask in range(1, groups)]
    docs = doc_lengths.shape[1]
    best = pl.pallas_call(
        functools.partial(score_kernel, groups),
        out_shape=jax.ShapeDtypeStruct((devices, groups, docs, 128), jnp.bfloat16),
        in_specs=[vmem] * (1 + groups),
        out_specs=vmem,
        compiler_params=params,
    )(plane, *blocks)
    met = lax.all_to_all(best, "dev", split_axis=0, concat_axis=0, tiled=True)
    scores = pl.pallas_call(
        functools.partial(pick_kernel, query_len),
        out_shape=jax.ShapeDtypeStruct(candidates.shape, jnp.float32),
        in_specs=[vmem, vmem],
        out_specs=vmem,
        compiler_params=params,
    )(candidates, met)
    return (vectors, scores)


def solution(mesh):
    placed = (
        P(("group", "dev"), None),
        P(),
        P("dev", None),
        P("dev", None),
        P(),
        P(),
        P(("group", "dev"), None, None),
        P("group", None),
        P(("group", "dev"), None),
    )
    return jax.shard_map(
        body,
        mesh=mesh,
        in_specs=placed,
        out_specs=(P(("group", "dev"), None), P(("group", "dev"), None)),
        check_vma=False,
    )
```

```python
import functools

import jax
import jax.numpy as jnp
from jax import lax
from jax.experimental import pallas as pl
from jax.experimental.pallas import tpu as pltpu
from jax.sharding import PartitionSpec as P

VMEM_LIMIT = 20 * 1024 * 1024


def norm_rows(values, gain_row):
    center = jnp.mean(values, axis=-1, keepdims=True)
    shifted = values - center
    spread = jnp.mean(shifted * shifted, axis=-1, keepdims=True)
    return (shifted * lax.rsqrt(spread + 1e-05) * gain_row).astype(jnp.bfloat16)


def dot_nt(left, right):
    return lax.dot_general(
        left, right, (((1,), (1,)), ((), ())), preferred_element_type=jnp.float32
    )


def split_kernel(chips, wi_ref, query_ref, *refs):
    pieces, turned = refs[:chips], refs[chips]
    columns = wi_ref.shape[1]
    width = columns // 2
    part = width // chips
    chip = lax.axis_index("dev") // 2
    for start in range(0, columns, 128):
        turned[start : start + 128, :] = wi_ref[:, start : start + 128].T
    for step in range(chips):
        for half in range(2):
            first = pl.multiple_of(half * width + (chip ^ step) * part, 16)
            pieces[step][half * part : (half + 1) * part] = turned[pl.ds(first, part), :]
        pieces[step][2 * part :] = query_ref[...]


def join_kernel(chips, wo_mine, wo_other, *refs):
    mine, other = refs[:chips], refs[chips : 2 * chips]
    gelu_w, gate_w, wo_part, queries = refs[2 * chips :]
    chip, core = lax.axis_index("dev") // 2, lax.axis_index("dev") % 2
    rows = wo_mine.shape[0]
    for first, upper, lower in ((0, wo_mine, wo_other), (1, wo_other, wo_mine)):

        @pl.when(core == first)
        def _(upper=upper, lower=lower):
            wo_part[:rows] = upper[...]
            wo_part[rows:] = lower[...]

    part = gelu_w.shape[0]
    own = mine[0].shape[0] - 2 * part
    for step in range(chips):
        source = (chip ^ step) * 2
        for block, at in ((mine[step], source + core), (other[step], source + 1 - core)):
            columns = pl.ds(pl.multiple_of(at * 128, 128), 128)
            gelu_w[:, columns] = block[:part]
            gate_w[:, columns] = block[part : 2 * part]
            queries[pl.ds(pl.multiple_of(at * own, own), own), :] = block[2 * part :]


def ffn_kernel(gain_ref, gelu_w, gate_w, wo_part, tokens_ref, out_ref):
    normed = norm_rows(tokens_ref[...].astype(jnp.float32), gain_ref[...])
    first = dot_nt(normed, gelu_w[...])
    second = dot_nt(normed, gate_w[...])
    hidden = (0.5 * first * (1.0 + lax.erf(first * 0.7071067811865476)) * second).astype(jnp.bfloat16)
    out_ref[...] = jnp.dot(hidden, wo_part[...], preferred_element_type=jnp.float32).astype(
        out_ref.dtype
    )


def far_order(groups):
    masks = list(range(1, groups))
    return masks[2:] + masks[:1] + masks[1:2]


def finish_kernel(chips, lengths_ref, tokens_ref, gain_ref, proj_ref, own_ref, *refs):
    parts, refs = refs[: chips - 1], refs[chips - 1 :]
    queries, (vectors_ref, out_ref) = refs[:-2], refs[-2:]
    mixed = tokens_ref[...].astype(jnp.float32) + own_ref[...]
    for part in parts:
        mixed = mixed + part[...].astype(jnp.float32)
    final = norm_rows(mixed, gain_ref[...])
    projected = jnp.dot(final, proj_ref[...], preferred_element_type=jnp.float32)
    total = jnp.sum(projected * projected, axis=-1, keepdims=True)
    vectors = (projected * lax.rsqrt(total + 1e-06)).astype(jnp.bfloat16)
    vectors_ref[...] = vectors
    group, me = lax.axis_index("group"), lax.axis_index("dev")
    rows = vectors.shape[0]
    docs = out_ref.shape[1]
    spot = me * rows + lax.broadcasted_iota(jnp.int32, (rows, 128), 0)
    inside, low = [], jnp.int32(0)
    for doc in range(docs):
        high = low + lengths_ref[0, doc]
        inside.append((spot >= low) & (spot < high))
        low = high
    for far, block in zip([0, *far_order(len(queries))], queries):
        for start in range(0, block.shape[0], 128):
            similar = dot_nt(vectors, block[start : start + 128, :])
            best = [
                jnp.max(jnp.where(inside[doc], similar, -jnp.inf), axis=0, keepdims=True)
                for doc in range(docs)
            ]
            best = jnp.concatenate(best, axis=0).astype(jnp.bfloat16)
            target = (group ^ far) * (2 * chips) + start // 64
            out_ref[target] = best
            out_ref[target + 1] = best


def pick_kernel(query_len, cand_ref, best_ref, out_ref):
    groups, _, docs, lanes = best_ref.shape
    own, listed = cand_ref.shape
    offset = (lax.axis_index("dev") % 2) * own * query_len
    scores = [jnp.zeros((1, listed), jnp.float32) for _ in range(own)]
    lane = lax.broadcasted_iota(jnp.int32, (docs, lanes), 1)
    label = lax.broadcasted_iota(jnp.int32, (docs, listed), 0)
    for far in range(groups):
        best = jnp.max(best_ref[far].astype(jnp.float32), axis=0)
        for query in range(own):
            start = offset + query * query_len
            taken = jnp.where((lane >= start) & (lane < start + query_len), best, 0.0)
            value = jnp.sum(taken, axis=1, keepdims=True) / query_len
            wanted = cand_ref[query : query + 1, :] - far * docs
            scores[query] += jnp.sum(jnp.where(wanted == label, value, 0.0), axis=0, keepdims=True)
    for query in range(own):
        out_ref[query : query + 1, :] = scores[query]


def body(
    corpus_tokens,
    norm_gain,
    wi_weight,
    wo_weight,
    final_gain,
    proj_weight,
    query_vectors,
    doc_lengths,
    candidates,
):
    groups = lax.axis_size("group")
    devices = lax.axis_size("dev")
    chips = devices // 2
    rows, width = corpus_tokens.shape
    part = wo_weight.shape[0] * 2
    smem = pl.BlockSpec(memory_space=pltpu.SMEM)
    vmem = pl.BlockSpec(memory_space=pltpu.VMEM)
    params = pltpu.CompilerParams(vmem_limit_bytes=VMEM_LIMIT)

    def swap(values, mask, axis="dev"):
        size = devices if axis == "dev" else groups
        return lax.ppermute(values, axis, [(i, i ^ mask) for i in range(size)])

    per_query, query_len, vector_dim = query_vectors.shape
    query_own = query_vectors.reshape(-1, vector_dim)
    wo_other = swap(wo_weight, 1)
    tokens = [corpus_tokens] + [swap(corpus_tokens, 2 * step) for step in range(1, chips)]
    if wi_weight.shape[0] == 128 and part % 16 == 0:
        piece_shape = jax.ShapeDtypeStruct((2 * part + query_own.shape[0], 128), jnp.bfloat16)
        pieces = pl.pallas_call(
            functools.partial(split_kernel, chips),
            out_shape=[piece_shape] * chips,
            in_specs=[vmem] * 2,
            out_specs=[vmem] * chips,
            scratch_shapes=[pltpu.VMEM((wi_weight.shape[1], 128), jnp.bfloat16)],
            compiler_params=params,
        )(wi_weight, query_own)
        mine = [pieces[0]] + [swap(pieces[step], 2 * step) for step in range(1, chips)]
        mine[1], tokens[1], tokens[2] = lax.optimization_barrier((mine[1], tokens[1], tokens[2]))
        other = [swap(piece, 1) for piece in mine]
        *weights, plane = pl.pallas_call(
            functools.partial(join_kernel, chips),
            out_shape=[
                jax.ShapeDtypeStruct((part, width), jnp.bfloat16),
                jax.ShapeDtypeStruct((part, width), jnp.bfloat16),
                jax.ShapeDtypeStruct((part, wo_weight.shape[1]), jnp.bfloat16),
                jax.ShapeDtypeStruct((devices * query_own.shape[0], vector_dim), jnp.bfloat16),
            ],
            in_specs=[vmem] * (2 + 2 * chips),
            out_specs=[vmem] * 4,
            compiler_params=params,
        )(wo_weight, wo_other, *mine, *other)
    else:
        me = lax.axis_index("dev")
        whole = lax.all_gather(wi_weight, "dev", axis=0, tiled=True).reshape(width, 2, chips, part)
        columns = lax.dynamic_index_in_dim(whole, me // 2, 2, keepdims=False)
        even = (me % 2) == 0
        wo_part = jnp.concatenate(
            [jnp.where(even, wo_weight, wo_other), jnp.where(even, wo_other, wo_weight)], axis=0
        )
        weights = [columns[:, 0].T, columns[:, 1].T, wo_part]
        plane = lax.all_gather(query_own, "dev", axis=0, tiled=True)
    partial = [None] * chips
    for step in list(range(1, chips)) + [0]:
        partial[step] = pl.pallas_call(
            ffn_kernel,
            out_shape=jax.ShapeDtypeStruct((rows, width), jnp.bfloat16 if step else jnp.float32),
            in_specs=[vmem] * 5,
            out_specs=vmem,
            compiler_params=params,
        )(norm_gain.reshape(1, -1), *weights, tokens[step])
    arrived = [swap(partial[step], 2 * step) for step in range(1, chips)]
    queries = [plane] + [swap(plane, mask, "group") for mask in far_order(groups)]

    docs = doc_lengths.shape[1]
    vectors, best = pl.pallas_call(
        functools.partial(finish_kernel, chips),
        out_shape=[
            jax.ShapeDtypeStruct((rows, proj_weight.shape[1]), jnp.bfloat16),
            jax.ShapeDtypeStruct((groups * devices, docs, 128), jnp.bfloat16),
        ],
        in_specs=[smem] + [vmem] * (4 + chips - 1 + groups),
        out_specs=[vmem, vmem],
        compiler_params=params,
    )(
        doc_lengths,
        corpus_tokens,
        final_gain.reshape(1, -1),
        proj_weight,
        partial[0],
        *arrived[::-1],
        *queries,
    )
    met = lax.all_to_all(best, ("group", "dev"), split_axis=0, concat_axis=0, tiled=True)
    scores = pl.pallas_call(
        functools.partial(pick_kernel, query_len),
        out_shape=jax.ShapeDtypeStruct(candidates.shape, jnp.float32),
        in_specs=[vmem, vmem],
        out_specs=vmem,
        compiler_params=params,
    )(candidates, met.reshape(groups, devices, docs, 128))
    return (vectors, scores)


def solution(mesh):
    placed = (
        P(("group", "dev"), None),
        P(),
        P("dev", None),
        P("dev", None),
        P(),
        P(),
        P(("group", "dev"), None, None),
        P("group", None),
        P(("group", "dev"), None),
    )
    return jax.shard_map(
        body,
        mesh=mesh,
        in_specs=placed,
        out_specs=(P(("group", "dev"), None), P(("group", "dev"), None)),
        check_vma=False,
    )
```

```python
import functools

import jax
import jax.numpy as jnp
from jax import lax
from jax.experimental import pallas as pl
from jax.experimental.pallas import tpu as pltpu
from jax.sharding import PartitionSpec as P

VMEM_LIMIT = 20 * 1024 * 1024


def norm_rows(values, gain_row):
    center = jnp.mean(values, axis=-1, keepdims=True)
    shifted = values - center
    spread = jnp.mean(shifted * shifted, axis=-1, keepdims=True)
    return (shifted * lax.rsqrt(spread + 1e-05) * gain_row).astype(jnp.bfloat16)


def dot_nt(left, right):
    return lax.dot_general(
        left, right, (((1,), (1,)), ((), ())), preferred_element_type=jnp.float32
    )


def split_kernel(chips, wi_ref, query_ref, *refs):
    pieces, turned = refs[:chips], refs[chips]
    columns = wi_ref.shape[1]
    width = columns // 2
    part = width // chips
    chip = lax.axis_index("dev") // 2
    for start in range(0, columns, 128):
        turned[start : start + 128, :] = wi_ref[:, start : start + 128].T
    for step in range(chips):
        halves = (0, 1) if step < 3 else (lax.axis_index("group") % 2,)
        for at, half in enumerate(halves):
            first = pl.multiple_of(half * width + (chip ^ step) * part, 16)
            pieces[step][at * part : (at + 1) * part] = turned[pl.ds(first, part), :]
        pieces[step][len(halves) * part :] = query_ref[...]


def join_kernel(chips, wo_mine, wo_other, *refs):
    mine, other = refs[: chips + 1], refs[chips + 1 : 2 * chips + 2]
    gelu_w, gate_w, wo_part, queries = refs[2 * chips + 2 :]
    chip, core = lax.axis_index("dev") // 2, lax.axis_index("dev") % 2
    rows = wo_mine.shape[0]
    for first, upper, lower in ((0, wo_mine, wo_other), (1, wo_other, wo_mine)):

        @pl.when(core == first)
        def _(upper=upper, lower=lower):
            wo_part[:rows] = upper[...]
            wo_part[rows:] = lower[...]

    part = gelu_w.shape[0]
    own = mine[0].shape[0] - 2 * part
    for step in range(chips):
        source = (chip ^ step) * 2
        for blocks, at in ((mine, source + core), (other, source + 1 - core)):
            columns = pl.ds(pl.multiple_of(at * 128, 128), 128)
            if step < 3:
                gelu_w[:, columns] = blocks[step][:part]
                gate_w[:, columns] = blocks[step][part : 2 * part]
            else:
                for parity in range(2):

                    @pl.when(lax.axis_index("group") % 2 == parity)
                    def _(parity=parity, blocks=blocks, columns=columns):
                        gelu_w[:, columns] = blocks[3 + parity][:part]
                        gate_w[:, columns] = blocks[4 - parity][:part]

            last = 2 * part if step < 3 else part
            queries[pl.ds(pl.multiple_of(at * own, own), own), :] = blocks[step][last : last + own]


def ffn_kernel(gain_ref, gelu_w, gate_w, wo_part, tokens_ref, out_ref):
    normed = norm_rows(tokens_ref[...].astype(jnp.float32), gain_ref[...])
    first = dot_nt(normed, gelu_w[...])
    second = dot_nt(normed, gate_w[...])
    hidden = (0.5 * first * (1.0 + lax.erf(first * 0.7071067811865476)) * second).astype(jnp.bfloat16)
    out_ref[...] = jnp.dot(hidden, wo_part[...], preferred_element_type=jnp.float32).astype(
        out_ref.dtype
    )


def far_order(groups):
    masks = list(range(1, groups))
    return masks[2:] + masks[:1] + masks[1:2]


def finish_kernel(chips, lengths_ref, tokens_ref, gain_ref, proj_ref, own_ref, *refs):
    parts, refs = refs[: chips - 1], refs[chips - 1 :]
    queries, (vectors_ref, out_ref) = refs[:-2], refs[-2:]
    mixed = tokens_ref[...].astype(jnp.float32) + own_ref[...]
    for part in parts:
        mixed = mixed + part[...].astype(jnp.float32)
    final = norm_rows(mixed, gain_ref[...])
    projected = jnp.dot(final, proj_ref[...], preferred_element_type=jnp.float32)
    total = jnp.sum(projected * projected, axis=-1, keepdims=True)
    vectors = (projected * lax.rsqrt(total + 1e-06)).astype(jnp.bfloat16)
    vectors_ref[...] = vectors
    group, me = lax.axis_index("group"), lax.axis_index("dev")
    rows = vectors.shape[0]
    docs = out_ref.shape[1]
    spot = me * rows + lax.broadcasted_iota(jnp.int32, (rows, 128), 0)
    inside, low = [], jnp.int32(0)
    for doc in range(docs):
        high = low + lengths_ref[0, doc]
        inside.append((spot >= low) & (spot < high))
        low = high
    for far, block in zip([0, *far_order(len(queries))], queries):
        for start in range(0, block.shape[0], 128):
            similar = dot_nt(vectors, block[start : start + 128, :])
            best = [
                jnp.max(jnp.where(inside[doc], similar, -jnp.inf), axis=0, keepdims=True)
                for doc in range(docs)
            ]
            best = jnp.concatenate(best, axis=0).astype(jnp.bfloat16)
            target = (group ^ far) * (2 * chips) + start // 64
            out_ref[target] = best
            out_ref[target + 1] = best


def pick_kernel(query_len, cand_ref, best_ref, out_ref):
    groups, _, docs, lanes = best_ref.shape
    own, listed = cand_ref.shape
    offset = (lax.axis_index("dev") % 2) * own * query_len
    scores = [jnp.zeros((1, listed), jnp.float32) for _ in range(own)]
    lane = lax.broadcasted_iota(jnp.int32, (docs, lanes), 1)
    label = lax.broadcasted_iota(jnp.int32, (docs, listed), 0)
    for far in range(groups):
        best = jnp.max(best_ref[far].astype(jnp.float32), axis=0)
        for query in range(own):
            start = offset + query * query_len
            taken = jnp.where((lane >= start) & (lane < start + query_len), best, 0.0)
            value = jnp.sum(taken, axis=1, keepdims=True) / query_len
            wanted = cand_ref[query : query + 1, :] - far * docs
            scores[query] += jnp.sum(jnp.where(wanted == label, value, 0.0), axis=0, keepdims=True)
    for query in range(own):
        out_ref[query : query + 1, :] = scores[query]


def body(
    corpus_tokens,
    norm_gain,
    wi_weight,
    wo_weight,
    final_gain,
    proj_weight,
    query_vectors,
    doc_lengths,
    candidates,
):
    groups = lax.axis_size("group")
    devices = lax.axis_size("dev")
    chips = devices // 2
    rows, width = corpus_tokens.shape
    part = wo_weight.shape[0] * 2
    smem = pl.BlockSpec(memory_space=pltpu.SMEM)
    vmem = pl.BlockSpec(memory_space=pltpu.VMEM)
    params = pltpu.CompilerParams(vmem_limit_bytes=VMEM_LIMIT)

    def swap(values, mask, axis="dev"):
        size = devices if axis == "dev" else groups
        return lax.ppermute(values, axis, [(i, i ^ mask) for i in range(size)])

    per_query, query_len, vector_dim = query_vectors.shape
    query_own = query_vectors.reshape(-1, vector_dim)
    wo_other = swap(wo_weight, 1)
    tokens = [corpus_tokens] + [swap(corpus_tokens, 2 * step) for step in range(1, chips)]
    if wi_weight.shape[0] == 128 and part % 16 == 0 and chips == 4 and groups % 2 == 0:
        own = query_own.shape[0]
        pieces = pl.pallas_call(
            functools.partial(split_kernel, chips),
            out_shape=[
                jax.ShapeDtypeStruct(((2 if step < 3 else 1) * part + own, 128), jnp.bfloat16)
                for step in range(chips)
            ],
            in_specs=[vmem] * 2,
            out_specs=[vmem] * chips,
            scratch_shapes=[pltpu.VMEM((wi_weight.shape[1], 128), jnp.bfloat16)],
            compiler_params=params,
        )(wi_weight, query_own)
        mine = [pieces[0]] + [swap(pieces[step], 2 * step) for step in range(1, chips)]
        mine.append(swap(mine[3], 1, "group"))
        mine[1], mine[4], tokens[1], tokens[2] = lax.optimization_barrier(
            (mine[1], mine[4], tokens[1], tokens[2])
        )
        other = [swap(piece, 1) for piece in mine]
        *weights, plane = pl.pallas_call(
            functools.partial(join_kernel, chips),
            out_shape=[
                jax.ShapeDtypeStruct((part, width), jnp.bfloat16),
                jax.ShapeDtypeStruct((part, width), jnp.bfloat16),
                jax.ShapeDtypeStruct((part, wo_weight.shape[1]), jnp.bfloat16),
                jax.ShapeDtypeStruct((devices * own, vector_dim), jnp.bfloat16),
            ],
            in_specs=[vmem] * (4 + 2 * chips),
            out_specs=[vmem] * 4,
            compiler_params=params,
        )(wo_weight, wo_other, *mine, *other)
    else:
        me = lax.axis_index("dev")
        whole = lax.all_gather(wi_weight, "dev", axis=0, tiled=True).reshape(width, 2, chips, part)
        columns = lax.dynamic_index_in_dim(whole, me // 2, 2, keepdims=False)
        even = (me % 2) == 0
        wo_part = jnp.concatenate(
            [jnp.where(even, wo_weight, wo_other), jnp.where(even, wo_other, wo_weight)], axis=0
        )
        weights = [columns[:, 0].T, columns[:, 1].T, wo_part]
        plane = lax.all_gather(query_own, "dev", axis=0, tiled=True)
    partial = [None] * chips
    for step in list(range(1, chips)) + [0]:
        partial[step] = pl.pallas_call(
            ffn_kernel,
            out_shape=jax.ShapeDtypeStruct((rows, width), jnp.bfloat16 if step else jnp.float32),
            in_specs=[vmem] * 5,
            out_specs=vmem,
            compiler_params=params,
        )(norm_gain.reshape(1, -1), *weights, tokens[step])
    arrived = [swap(partial[step], 2 * step) for step in range(1, chips)]
    queries = [plane] + [swap(plane, mask, "group") for mask in far_order(groups)]

    docs = doc_lengths.shape[1]
    vectors, best = pl.pallas_call(
        functools.partial(finish_kernel, chips),
        out_shape=[
            jax.ShapeDtypeStruct((rows, proj_weight.shape[1]), jnp.bfloat16),
            jax.ShapeDtypeStruct((groups * devices, docs, 128), jnp.bfloat16),
        ],
        in_specs=[smem] + [vmem] * (4 + chips - 1 + groups),
        out_specs=[vmem, vmem],
        compiler_params=params,
    )(
        doc_lengths,
        corpus_tokens,
        final_gain.reshape(1, -1),
        proj_weight,
        partial[0],
        *arrived[::-1],
        *queries,
    )
    met = lax.all_to_all(best, ("group", "dev"), split_axis=0, concat_axis=0, tiled=True)
    scores = pl.pallas_call(
        functools.partial(pick_kernel, query_len),
        out_shape=jax.ShapeDtypeStruct(candidates.shape, jnp.float32),
        in_specs=[vmem, vmem],
        out_specs=vmem,
        compiler_params=params,
    )(candidates, met.reshape(groups, devices, docs, 128))
    return (vectors, scores)


def solution(mesh):
    placed = (
        P(("group", "dev"), None),
        P(),
        P("dev", None),
        P("dev", None),
        P(),
        P(),
        P(("group", "dev"), None, None),
        P("group", None),
        P(("group", "dev"), None),
    )
    return jax.shard_map(
        body,
        mesh=mesh,
        in_specs=placed,
        out_specs=(P(("group", "dev"), None), P(("group", "dev"), None)),
        check_vma=False,
    )
```

```python
import functools

import jax
import jax.numpy as jnp
from jax import lax
from jax.experimental import pallas as pl
from jax.experimental.pallas import tpu as pltpu
from jax.sharding import PartitionSpec as P

VMEM_LIMIT = 20 * 1024 * 1024


def norm_rows(values, gain_row):
    center = jnp.mean(values, axis=-1, keepdims=True)
    shifted = values - center
    spread = jnp.mean(shifted * shifted, axis=-1, keepdims=True)
    return (shifted * lax.rsqrt(spread + 1e-05) * gain_row).astype(jnp.bfloat16)


def dot_nt(left, right):
    return lax.dot_general(
        left, right, (((1,), (1,)), ((), ())), preferred_element_type=jnp.float32
    )


def split_kernel(chips, wi_ref, query_ref, *refs):
    pieces, turned = refs[:chips], refs[chips]
    columns = wi_ref.shape[1]
    width = columns // 2
    part = width // chips
    chip = lax.axis_index("dev") // 2
    for start in range(0, columns, 128):
        turned[start : start + 128, :] = wi_ref[:, start : start + 128].T
    for step in range(chips):
        halves = (0, 1) if step < 3 else (lax.axis_index("group") % 2,)
        for at, half in enumerate(halves):
            first = pl.multiple_of(half * width + (chip ^ step) * part, 16)
            pieces[step][at * part : (at + 1) * part] = turned[pl.ds(first, part), :]
        pieces[step][len(halves) * part :] = query_ref[...]


def join_kernel(chips, wo_mine, wo_other, *refs):
    mine, other = refs[: chips + 1], refs[chips + 1 : 2 * chips + 2]
    gelu_w, gate_w, wo_part, queries = refs[2 * chips + 2 :]
    chip, core = lax.axis_index("dev") // 2, lax.axis_index("dev") % 2
    rows = wo_mine.shape[0]
    for first, upper, lower in ((0, wo_mine, wo_other), (1, wo_other, wo_mine)):

        @pl.when(core == first)
        def _(upper=upper, lower=lower):
            wo_part[:rows] = upper[...]
            wo_part[rows:] = lower[...]

    part = gelu_w.shape[0]
    own = mine[0].shape[0] - 2 * part
    for step in range(chips):
        source = (chip ^ step) * 2
        for blocks, at in ((mine, source + core), (other, source + 1 - core)):
            columns = pl.ds(pl.multiple_of(at * 128, 128), 128)
            if step < 3:
                gelu_w[:, columns] = blocks[step][:part]
                gate_w[:, columns] = blocks[step][part : 2 * part]
            else:
                for parity in range(2):

                    @pl.when(lax.axis_index("group") % 2 == parity)
                    def _(parity=parity, blocks=blocks, columns=columns):
                        gelu_w[:, columns] = blocks[3 + parity][:part]
                        gate_w[:, columns] = blocks[4 - parity][:part]

            last = 2 * part if step < 3 else part
            queries[pl.ds(pl.multiple_of(at * own, own), own), :] = blocks[step][last : last + own]


def ffn_kernel(gain_ref, gelu_w, gate_w, wo_part, tokens_ref, out_ref):
    normed = norm_rows(tokens_ref[...].astype(jnp.float32), gain_ref[...])
    first = dot_nt(normed, gelu_w[...])
    second = dot_nt(normed, gate_w[...])
    hidden = (0.5 * first * (1.0 + lax.erf(first * 0.7071067811865476)) * second).astype(jnp.bfloat16)
    out_ref[...] = jnp.dot(hidden, wo_part[...], preferred_element_type=jnp.float32).astype(
        out_ref.dtype
    )


def far_order(groups):
    masks = list(range(1, groups))
    return masks[2:] + masks[:1] + masks[1:2]


def finish_kernel(chips, lengths_ref, tokens_ref, gain_ref, proj_ref, own_ref, *refs):
    parts, refs = refs[: chips - 1], refs[chips - 1 :]
    queries, (vectors_ref, out_ref) = refs[:-2], refs[-2:]
    mixed = tokens_ref[...].astype(jnp.float32) + own_ref[...]
    for part in parts:
        mixed = mixed + part[...].astype(jnp.float32)
    final = norm_rows(mixed, gain_ref[...])
    projected = jnp.dot(final, proj_ref[...], preferred_element_type=jnp.float32)
    total = jnp.sum(projected * projected, axis=-1, keepdims=True)
    vectors = (projected * lax.rsqrt(total + 1e-06)).astype(jnp.bfloat16)
    vectors_ref[...] = vectors
    group, me = lax.axis_index("group"), lax.axis_index("dev")
    rows = vectors.shape[0]
    docs = out_ref.shape[1]
    spot = me * rows + lax.broadcasted_iota(jnp.int32, (rows, 128), 0)
    inside, low = [], jnp.int32(0)
    for doc in range(docs):
        high = low + lengths_ref[0, doc]
        inside.append((spot >= low) & (spot < high))
        low = high
    for far, block in zip([0, *far_order(len(queries))], queries):
        for start in range(0, block.shape[0], 128):
            similar = dot_nt(vectors, block[start : start + 128, :])
            best = [
                jnp.max(jnp.where(inside[doc], similar, -jnp.inf), axis=0, keepdims=True)
                for doc in range(docs)
            ]
            best = jnp.concatenate(best, axis=0).astype(jnp.bfloat16)
            target = (group ^ far) * (2 * chips) + start // 64
            out_ref[target] = best
            out_ref[target + 1] = best


def pick_kernel(query_len, cand_ref, best_ref, out_ref):
    groups, _, docs, lanes = best_ref.shape
    own, listed = cand_ref.shape
    offset = (lax.axis_index("dev") % 2) * own * query_len
    scores = [jnp.zeros((1, listed), jnp.float32) for _ in range(own)]
    lane = lax.broadcasted_iota(jnp.int32, (docs, lanes), 1)
    label = lax.broadcasted_iota(jnp.int32, (docs, listed), 0)
    for far in range(groups):
        best = jnp.max(best_ref[far].astype(jnp.float32), axis=0)
        for query in range(own):
            start = offset + query * query_len
            taken = jnp.where((lane >= start) & (lane < start + query_len), best, 0.0)
            value = jnp.sum(taken, axis=1, keepdims=True) / query_len
            wanted = cand_ref[query : query + 1, :] - far * docs
            scores[query] += jnp.sum(jnp.where(wanted == label, value, 0.0), axis=0, keepdims=True)
    for query in range(own):
        out_ref[query : query + 1, :] = scores[query]


def body(
    corpus_tokens,
    norm_gain,
    wi_weight,
    wo_weight,
    final_gain,
    proj_weight,
    query_vectors,
    doc_lengths,
    candidates,
):
    groups = lax.axis_size("group")
    devices = lax.axis_size("dev")
    chips = devices // 2
    rows, width = corpus_tokens.shape
    part = wo_weight.shape[0] * 2
    smem = pl.BlockSpec(memory_space=pltpu.SMEM)
    vmem = pl.BlockSpec(memory_space=pltpu.VMEM)
    params = pltpu.CompilerParams(vmem_limit_bytes=VMEM_LIMIT)

    def swap(values, mask, axis="dev"):
        size = devices if axis == "dev" else groups
        return lax.ppermute(values, axis, [(i, i ^ mask) for i in range(size)])

    per_query, query_len, vector_dim = query_vectors.shape
    query_own = query_vectors.reshape(-1, vector_dim)
    wo_other = swap(wo_weight, 1)
    tokens = [corpus_tokens] + [swap(corpus_tokens, 2 * step) for step in range(1, chips)]
    if wi_weight.shape[0] == 128 and part % 16 == 0 and chips == 4 and groups % 2 == 0:
        own = query_own.shape[0]
        pieces = pl.pallas_call(
            functools.partial(split_kernel, chips),
            out_shape=[
                jax.ShapeDtypeStruct(((2 if step < 3 else 1) * part + own, 128), jnp.bfloat16)
                for step in range(chips)
            ],
            in_specs=[vmem] * 2,
            out_specs=[vmem] * chips,
            scratch_shapes=[pltpu.VMEM((wi_weight.shape[1], 128), jnp.bfloat16)],
            compiler_params=params,
        )(wi_weight, query_own)
        mine = [pieces[0]] + [swap(pieces[step], 2 * step) for step in range(1, chips)]
        mine[3], tokens[1], tokens[2] = lax.optimization_barrier((mine[3], tokens[1], tokens[2]))
        mine.append(swap(mine[3], 1, "group"))
        mine[0], mine[1], mine[4], tokens[1], tokens[2] = lax.optimization_barrier(
            (mine[0], mine[1], mine[4], tokens[1], tokens[2])
        )
        other = [swap(piece, 1) for piece in mine]
        *weights, plane = pl.pallas_call(
            functools.partial(join_kernel, chips),
            out_shape=[
                jax.ShapeDtypeStruct((part, width), jnp.bfloat16),
                jax.ShapeDtypeStruct((part, width), jnp.bfloat16),
                jax.ShapeDtypeStruct((part, wo_weight.shape[1]), jnp.bfloat16),
                jax.ShapeDtypeStruct((devices * own, vector_dim), jnp.bfloat16),
            ],
            in_specs=[vmem] * (4 + 2 * chips),
            out_specs=[vmem] * 4,
            compiler_params=params,
        )(wo_weight, wo_other, *mine, *other)
    else:
        me = lax.axis_index("dev")
        whole = lax.all_gather(wi_weight, "dev", axis=0, tiled=True).reshape(width, 2, chips, part)
        columns = lax.dynamic_index_in_dim(whole, me // 2, 2, keepdims=False)
        even = (me % 2) == 0
        wo_part = jnp.concatenate(
            [jnp.where(even, wo_weight, wo_other), jnp.where(even, wo_other, wo_weight)], axis=0
        )
        weights = [columns[:, 0].T, columns[:, 1].T, wo_part]
        plane = lax.all_gather(query_own, "dev", axis=0, tiled=True)
    partial = [None] * chips
    for step in list(range(1, chips)) + [0]:
        partial[step] = pl.pallas_call(
            ffn_kernel,
            out_shape=jax.ShapeDtypeStruct((rows, width), jnp.bfloat16 if step else jnp.float32),
            in_specs=[vmem] * 5,
            out_specs=vmem,
            compiler_params=params,
        )(norm_gain.reshape(1, -1), *weights, tokens[step])
    arrived = [swap(partial[step], 2 * step) for step in range(1, chips)]
    queries = [plane] + [swap(plane, mask, "group") for mask in far_order(groups)]

    docs = doc_lengths.shape[1]
    vectors, best = pl.pallas_call(
        functools.partial(finish_kernel, chips),
        out_shape=[
            jax.ShapeDtypeStruct((rows, proj_weight.shape[1]), jnp.bfloat16),
            jax.ShapeDtypeStruct((groups * devices, docs, 128), jnp.bfloat16),
        ],
        in_specs=[smem] + [vmem] * (4 + chips - 1 + groups),
        out_specs=[vmem, vmem],
        compiler_params=params,
    )(
        doc_lengths,
        corpus_tokens,
        final_gain.reshape(1, -1),
        proj_weight,
        partial[0],
        *arrived[::-1],
        *queries,
    )
    met = lax.all_to_all(best, ("group", "dev"), split_axis=0, concat_axis=0, tiled=True)
    scores = pl.pallas_call(
        functools.partial(pick_kernel, query_len),
        out_shape=jax.ShapeDtypeStruct(candidates.shape, jnp.float32),
        in_specs=[vmem, vmem],
        out_specs=vmem,
        compiler_params=params,
    )(candidates, met.reshape(groups, devices, docs, 128))
    return (vectors, scores)


def solution(mesh):
    placed = (
        P(("group", "dev"), None),
        P(),
        P("dev", None),
        P("dev", None),
        P(),
        P(),
        P(("group", "dev"), None, None),
        P("group", None),
        P(("group", "dev"), None),
    )
    return jax.shard_map(
        body,
        mesh=mesh,
        in_specs=placed,
        out_specs=(P(("group", "dev"), None), P(("group", "dev"), None)),
        check_vma=False,
    )
```

```python
import functools

import jax
import jax.numpy as jnp
from jax import lax
from jax.experimental import pallas as pl
from jax.experimental.pallas import tpu as pltpu
from jax.sharding import PartitionSpec as P

VMEM_LIMIT = 20 * 1024 * 1024


def norm_rows(values, gain_row):
    center = jnp.mean(values, axis=-1, keepdims=True)
    shifted = values - center
    spread = jnp.mean(shifted * shifted, axis=-1, keepdims=True)
    return (shifted * lax.rsqrt(spread + 1e-05) * gain_row).astype(jnp.bfloat16)


def dot_nt(left, right):
    return lax.dot_general(
        left, right, (((1,), (1,)), ((), ())), preferred_element_type=jnp.float32
    )


def split_kernel(chips, wi_ref, query_ref, *refs):
    pieces, turned = refs[:chips], refs[chips]
    columns = wi_ref.shape[1]
    width = columns // 2
    part = width // chips
    chip = lax.axis_index("dev") // 2
    for start in range(0, columns, 128):
        turned[start : start + 128, :] = wi_ref[:, start : start + 128].T
    for step in range(chips):
        halves = (0, 1) if step < 3 else (lax.axis_index("group") % 2,)
        for at, half in enumerate(halves):
            first = pl.multiple_of(half * width + (chip ^ step) * part, 16)
            pieces[step][at * part : (at + 1) * part] = turned[pl.ds(first, part), :]
        pieces[step][len(halves) * part :] = query_ref[...]


def join_kernel(chips, wo_mine, wo_other, *refs):
    mine, other = refs[: chips + 1], refs[chips + 1 : 2 * chips + 2]
    gelu_w, gate_w, wo_part, queries = refs[2 * chips + 2 :]
    chip, core = lax.axis_index("dev") // 2, lax.axis_index("dev") % 2
    rows = wo_mine.shape[0]
    for first, upper, lower in ((0, wo_mine, wo_other), (1, wo_other, wo_mine)):

        @pl.when(core == first)
        def _(upper=upper, lower=lower):
            wo_part[:rows] = upper[...]
            wo_part[rows:] = lower[...]

    part = gelu_w.shape[0]
    own = mine[0].shape[0] - 2 * part
    for step in range(chips):
        source = (chip ^ step) * 2
        for blocks, at in ((mine, source + core), (other, source + 1 - core)):
            columns = pl.ds(pl.multiple_of(at * 128, 128), 128)
            if step < 3:
                gelu_w[:, columns] = blocks[step][:part]
                gate_w[:, columns] = blocks[step][part : 2 * part]
            else:
                for parity in range(2):

                    @pl.when(lax.axis_index("group") % 2 == parity)
                    def _(parity=parity, blocks=blocks, columns=columns):
                        gelu_w[:, columns] = blocks[3 + parity][:part]
                        gate_w[:, columns] = blocks[4 - parity][:part]

            last = 2 * part if step < 3 else part
            queries[pl.ds(pl.multiple_of(at * own, own), own), :] = blocks[step][last : last + own]


def ffn_kernel(gain_ref, gelu_w, gate_w, wo_part, tokens_ref, out_ref):
    normed = norm_rows(tokens_ref[...].astype(jnp.float32), gain_ref[...])
    first = dot_nt(normed, gelu_w[...])
    second = dot_nt(normed, gate_w[...])
    hidden = (0.5 * first * (1.0 + lax.erf(first * 0.7071067811865476)) * second).astype(jnp.bfloat16)
    out_ref[...] = jnp.dot(hidden, wo_part[...], preferred_element_type=jnp.float32).astype(
        out_ref.dtype
    )


def far_order(groups):
    masks = list(range(1, groups))
    return masks[1:2] + masks[:1] + masks[2:]


def finish_kernel(chips, lengths_ref, tokens_ref, gain_ref, proj_ref, own_ref, *refs):
    parts, refs = refs[: chips - 1], refs[chips - 1 :]
    queries, (vectors_ref, out_ref) = refs[:-2], refs[-2:]
    mixed = tokens_ref[...].astype(jnp.float32) + own_ref[...]
    for part in parts:
        mixed = mixed + part[...].astype(jnp.float32)
    final = norm_rows(mixed, gain_ref[...])
    projected = jnp.dot(final, proj_ref[...], preferred_element_type=jnp.float32)
    total = jnp.sum(projected * projected, axis=-1, keepdims=True)
    vectors = (projected * lax.rsqrt(total + 1e-06)).astype(jnp.bfloat16)
    vectors_ref[...] = vectors
    group, me = lax.axis_index("group"), lax.axis_index("dev")
    rows = vectors.shape[0]
    docs = out_ref.shape[1]
    spot = me * rows + lax.broadcasted_iota(jnp.int32, (rows, 128), 0)
    inside, low = [], jnp.int32(0)
    for doc in range(docs):
        high = low + lengths_ref[0, doc]
        inside.append((spot >= low) & (spot < high))
        low = high
    for far, block in zip([0, *far_order(len(queries))], queries):
        for start in range(0, block.shape[0], 128):
            similar = dot_nt(vectors, block[start : start + 128, :])
            best = [
                jnp.max(jnp.where(inside[doc], similar, -jnp.inf), axis=0, keepdims=True)
                for doc in range(docs)
            ]
            best = jnp.concatenate(best, axis=0).astype(jnp.bfloat16)
            target = (group ^ far) * (2 * chips) + start // 64
            out_ref[target] = best
            out_ref[target + 1] = best


def pick_kernel(query_len, cand_ref, best_ref, out_ref):
    groups, _, docs, lanes = best_ref.shape
    own, listed = cand_ref.shape
    offset = (lax.axis_index("dev") % 2) * own * query_len
    scores = [jnp.zeros((1, listed), jnp.float32) for _ in range(own)]
    lane = lax.broadcasted_iota(jnp.int32, (docs, lanes), 1)
    label = lax.broadcasted_iota(jnp.int32, (docs, listed), 0)
    for far in range(groups):
        best = jnp.max(best_ref[far].astype(jnp.float32), axis=0)
        for query in range(own):
            start = offset + query * query_len
            taken = jnp.where((lane >= start) & (lane < start + query_len), best, 0.0)
            value = jnp.sum(taken, axis=1, keepdims=True) / query_len
            wanted = cand_ref[query : query + 1, :] - far * docs
            scores[query] += jnp.sum(jnp.where(wanted == label, value, 0.0), axis=0, keepdims=True)
    for query in range(own):
        out_ref[query : query + 1, :] = scores[query]


def body(
    corpus_tokens,
    norm_gain,
    wi_weight,
    wo_weight,
    final_gain,
    proj_weight,
    query_vectors,
    doc_lengths,
    candidates,
):
    groups = lax.axis_size("group")
    devices = lax.axis_size("dev")
    chips = devices // 2
    rows, width = corpus_tokens.shape
    part = wo_weight.shape[0] * 2
    smem = pl.BlockSpec(memory_space=pltpu.SMEM)
    vmem = pl.BlockSpec(memory_space=pltpu.VMEM)
    params = pltpu.CompilerParams(vmem_limit_bytes=VMEM_LIMIT)

    def swap(values, mask, axis="dev"):
        size = devices if axis == "dev" else groups
        return lax.ppermute(values, axis, [(i, i ^ mask) for i in range(size)])

    per_query, query_len, vector_dim = query_vectors.shape
    query_own = query_vectors.reshape(-1, vector_dim)
    wo_other = swap(wo_weight, 1)
    tokens = [corpus_tokens] + [swap(corpus_tokens, 2 * step) for step in range(1, chips)]
    if wi_weight.shape[0] == 128 and part % 16 == 0 and chips == 4 and groups % 2 == 0:
        own = query_own.shape[0]
        pieces = pl.pallas_call(
            functools.partial(split_kernel, chips),
            out_shape=[
                jax.ShapeDtypeStruct(((2 if step < 3 else 1) * part + own, 128), jnp.bfloat16)
                for step in range(chips)
            ],
            in_specs=[vmem] * 2,
            out_specs=[vmem] * chips,
            scratch_shapes=[pltpu.VMEM((wi_weight.shape[1], 128), jnp.bfloat16)],
            compiler_params=params,
        )(wi_weight, query_own)
        mine = [pieces[0]] + [swap(pieces[step], 2 * step) for step in range(1, chips)]
        mine[3], tokens[1], tokens[2] = lax.optimization_barrier((mine[3], tokens[1], tokens[2]))
        mine.append(swap(mine[3], 1, "group"))
        mine[0], mine[1], mine[4], tokens[1], tokens[2] = lax.optimization_barrier(
            (mine[0], mine[1], mine[4], tokens[1], tokens[2])
        )
        other = [swap(piece, 1) for piece in mine]
        *weights, plane = pl.pallas_call(
            functools.partial(join_kernel, chips),
            out_shape=[
                jax.ShapeDtypeStruct((part, width), jnp.bfloat16),
                jax.ShapeDtypeStruct((part, width), jnp.bfloat16),
                jax.ShapeDtypeStruct((part, wo_weight.shape[1]), jnp.bfloat16),
                jax.ShapeDtypeStruct((devices * own, vector_dim), jnp.bfloat16),
            ],
            in_specs=[vmem] * (4 + 2 * chips),
            out_specs=[vmem] * 4,
            compiler_params=params,
        )(wo_weight, wo_other, *mine, *other)
    else:
        me = lax.axis_index("dev")
        whole = lax.all_gather(wi_weight, "dev", axis=0, tiled=True).reshape(width, 2, chips, part)
        columns = lax.dynamic_index_in_dim(whole, me // 2, 2, keepdims=False)
        even = (me % 2) == 0
        wo_part = jnp.concatenate(
            [jnp.where(even, wo_weight, wo_other), jnp.where(even, wo_other, wo_weight)], axis=0
        )
        weights = [columns[:, 0].T, columns[:, 1].T, wo_part]
        plane = lax.all_gather(query_own, "dev", axis=0, tiled=True)
    partial = [None] * chips
    for step in list(range(1, chips)) + [0]:
        partial[step] = pl.pallas_call(
            ffn_kernel,
            out_shape=jax.ShapeDtypeStruct((rows, width), jnp.bfloat16 if step else jnp.float32),
            in_specs=[vmem] * 5,
            out_specs=vmem,
            compiler_params=params,
        )(norm_gain.reshape(1, -1), *weights, tokens[step])
    arrived = [swap(partial[step], 2 * step) for step in range(1, chips)]
    queries = [plane] + [swap(plane, mask, "group") for mask in far_order(groups)]

    docs = doc_lengths.shape[1]
    vectors, best = pl.pallas_call(
        functools.partial(finish_kernel, chips),
        out_shape=[
            jax.ShapeDtypeStruct((rows, proj_weight.shape[1]), jnp.bfloat16),
            jax.ShapeDtypeStruct((groups * devices, docs, 128), jnp.bfloat16),
        ],
        in_specs=[smem] + [vmem] * (4 + chips - 1 + groups),
        out_specs=[vmem, vmem],
        compiler_params=params,
    )(
        doc_lengths,
        corpus_tokens,
        final_gain.reshape(1, -1),
        proj_weight,
        partial[0],
        *arrived[::-1],
        *queries,
    )
    met = lax.all_to_all(best, ("group", "dev"), split_axis=0, concat_axis=0, tiled=True)
    scores = pl.pallas_call(
        functools.partial(pick_kernel, query_len),
        out_shape=jax.ShapeDtypeStruct(candidates.shape, jnp.float32),
        in_specs=[vmem, vmem],
        out_specs=vmem,
        compiler_params=params,
    )(candidates, met.reshape(groups, devices, docs, 128))
    return (vectors, scores)


def solution(mesh):
    placed = (
        P(("group", "dev"), None),
        P(),
        P("dev", None),
        P("dev", None),
        P(),
        P(),
        P(("group", "dev"), None, None),
        P("group", None),
        P(("group", "dev"), None),
    )
    return jax.shard_map(
        body,
        mesh=mesh,
        in_specs=placed,
        out_specs=(P(("group", "dev"), None), P(("group", "dev"), None)),
        check_vma=False,
    )
```
